256 devices in a mesh: sx: 8 (over z), sy: 16 (over y, x_hi, core), grp: 2 (over x_lo).
Axes of the slice: x: 4 (x_hi: 2, x_lo: 2; x = x_hi * 2 + x_lo), y: 4, z: 8, core: 2. Of those that a mesh axis runs over, the one named last changes fastest.
Arguments:
- velocity: float32 [3, 16, 256, 2048], P(None, 'grp', 'sx', 'sy'), may hold values from -6 to 6
- target_stress: float32 [6, 16, 256, 2048], P(None, 'grp', 'sx', 'sy'), may hold values from -6 to 6
- w_conv: bfloat16 [27, 128], replicated, may hold values from -1.25 to 1.25
- b_conv: float32 [128], replicated, may hold values from -3 to 3
- w_mix: bfloat16 [128, 128], replicated, may hold values from -0.5 to 0.5
- b_mix: float32 [128], replicated, may hold values from -3 to 3
- w_out: bfloat16 [128, 6], replicated, may hold values from -0.5 to 0.5
- plane_offsets: int32 [2, 8, 16, 2], P('grp', 'sx', 'sy'), may hold values from 0 to 7
- trainer_map: int32 [2, 8, 32, 1], P('grp', 'sx'), may hold values from 0 to 15; in each aligned block of 32 rows (0 to 31, 32 to 63, ..., all dimensions but the last counted through in order) at most 4 rows name the same one
Outputs:
- tendency: float32 [3, 16, 256, 2048], P(None, 'grp', 'sx', 'sy')
- grad_conv: float32 [27, 128], replicated
- grad_bconv: float32 [128], replicated
- grad_mix: float32 [128, 128], replicated
- grad_bmix: float32 [128], replicated
- grad_out: float32 [128, 6], replicated
The draws below stay inside these ranges and needn't reach their ends.
Inputs may be any that keep to these rules, and one draw needn't show every extreme that they name: `trainer_map`: within one row of tiles (one index of grp and sx) no trainer index is named by more than 4 samples, a bound that some block reaches.
All inputs are finite; a program needn't handle non-finite values.
Results may differ from the reference program's by a relative error of at most 0.004.
Values sent between devices are 32-bit elements; how exact they have to be, the bound alone decides.
A program may use at most 64 MiB of HBM per device.

```python
import math
import jax
import jax.numpy as jnp
import numpy as np
from jax import lax

CX = 32
CY = 128
PZ = 8
FEAT = 128
S = 2
CAP = 4
NX = 256
NY = 2048
NZ = 16
SAMPLES = 512
N_SX = 8
N_SY = 16
N_GRP = 2


def plant(drawn, stream_key, smallest, top_value):
    longest = drawn.shape.index(max(drawn.shape))
    spots = []
    for shift in (0, 1):
        where = [jax.random.randint(jax.random.fold_in(stream_key, axis), (), 0, length) for axis, length in enumerate(drawn.shape)]
        where[longest] = (where[longest] + shift) % drawn.shape[longest]
        spots.append(tuple(where))
    return drawn.at[spots[0]].set(smallest).at[spots[1]].set(top_value)


def shard_levels(own_key, dims, split, smallest, largest):
    def one(axis_at, blocks):
        draws = jax.random.uniform(jax.random.fold_in(jax.random.fold_in(own_key, 6), axis_at), (blocks,), jnp.float32, smallest / len(split), largest / len(split))
        return jnp.repeat(jnp.exp(draws), dims[axis_at] // blocks).reshape((-1,) + (1,) * (len(dims) - axis_at - 1))

    level = one(*split[0])
    for cut in split[1:]:
        level = level * one(*cut)
    return level


def deal_out(own_key, own, number, rows, amount, top, most, lean):
    sequence = jax.random.permutation(own_key, amount)
    crowded, usual = shares(amount, rows * top, most, lean, True), shares(amount, rows * top, most, lean, False)
    places = jnp.arange(amount)

    def named(sizes, rotation):
        used = int((sizes > 0).sum())
        fixed = max(1, used // 4)
        moved = fixed + (places - fixed + rotation * (used - fixed)) % max(1, amount - fixed)
        return jnp.zeros((amount,), jnp.int32).at[sequence[jnp.where(places < fixed, places, moved)]].set(jnp.asarray(sizes, jnp.int32))

    sizes = jnp.where(number % 4 == 0, named(crowded, number // 4), named(usual, number - number // 4 - 1))
    mixed = jax.random.permutation(jax.random.fold_in(own, 3), amount)
    donor, taker = mixed[0:amount // 2 * 2:2], mixed[1:amount // 2 * 2:2]
    slack = jnp.minimum(sizes[donor] - 1, most - sizes[taker]) // 2
    slack = jnp.where((donor == sequence[0]) | (taker == sequence[0]) | (sizes[taker] == 0), 0, jnp.maximum(slack, 0))
    moved = jax.random.randint(jax.random.fold_in(own, 4), (amount // 2,), 0, 1 << 20) % (slack + 1)
    sizes = sizes.at[donor].add(-moved).at[taker].add(moved)
    members = jnp.searchsorted(jnp.cumsum(sizes), jnp.arange(rows * top), side="right").astype(jnp.int32)
    listing = members.reshape(top, rows).T
    listing = listing[jax.random.permutation(jax.random.fold_in(own, 1), rows)]
    rotation = jax.random.randint(jax.random.fold_in(own, 2), (rows, 1), 0, top)
    return jnp.take_along_axis(listing, (jnp.arange(top)[None, :] + rotation) % top, axis=1)


def shares(amount, total, bound, lean, full):
    weights = [(1 << 20) // math.isqrt(grade ** lean) + 1 for grade in range(1, amount + 1)]
    largest = bound if full else min(bound, max(-(-total // amount), total * weights[0] // sum(weights)))
    least = 1 if total - largest >= amount - 1 else 0
    holding, spare = [largest] + [least] * (amount - 1), total - largest - least * (amount - 1)
    while spare > 0:
        candidates = [i for i in range(1, amount) if holding[i] < largest] or [i for i in range(1, amount) if holding[i] < bound]
        mass, budget = sum([weights[i] for i in candidates]), spare
        for i in candidates:
            extra = min(bound - holding[i], max(1, budget * weights[i] // mass), spare)
            holding[i] = holding[i] + extra
            spare = spare - extra
    return np.array(holding)


def gaussian(own_key, dims, spread, reach, cuts=(), held_as=jnp.bfloat16):
    entries = spread * jax.random.normal(own_key, dims, jnp.float32)
    if cuts:
        entries = entries * shard_levels(own_key, dims, cuts, -0.22, 0.18)
    return jnp.clip(entries, -reach, reach).astype(held_as)


def setup_inputs(seed: int = 0) -> dict:
    arg_keys = jax.random.split(jax.random.key(seed), 10)
    velocity = gaussian(arg_keys[0], (3, NZ, NX, NY), 1.0, 6.0, ((1, 2), (2, 8), (3, 16)), jnp.float32)
    target_stress = gaussian(arg_keys[1], (6, NZ, NX, NY), 1.0, 6.0, ((1, 2), (2, 8), (3, 16)), jnp.float32)
    w_conv = gaussian(arg_keys[2], (27, FEAT), 27 ** -0.5, 1.25)
    b_conv = gaussian(arg_keys[3], (FEAT,), 0.5, 3.0, (), jnp.float32)
    w_mix = gaussian(arg_keys[4], (FEAT, FEAT), FEAT ** -0.5, 0.5)
    b_mix = gaussian(arg_keys[5], (FEAT,), 0.5, 3.0, (), jnp.float32)
    w_out = gaussian(arg_keys[6], (FEAT, 6), FEAT ** -0.5, 0.5)
    plane_offsets = plant(jax.random.randint(arg_keys[7], (N_GRP, N_SX, N_SY, S), 0, PZ), jax.random.fold_in(arg_keys[7], 1), 0, PZ - 1).astype(jnp.int32)
    trainer_map_keys = jax.random.split(jax.random.fold_in(arg_keys[8], 1), N_GRP * N_SX * (N_SY * S) // (N_SY * S))
    trainer_map_turns = jax.random.permutation(jax.random.fold_in(arg_keys[8], 3), N_GRP * N_SX * (N_SY * S) // (N_SY * S))
    trainer_map = jax.vmap(lambda own, number: deal_out(jax.random.fold_in(arg_keys[8], 2), own, number, N_SY * S, N_SY, 1, CAP, 2))(trainer_map_keys, trainer_map_turns).reshape((N_GRP, N_SX, N_SY * S, 1))
    return dict(velocity=velocity, target_stress=target_stress, w_conv=w_conv, b_conv=b_conv, w_mix=w_mix, b_mix=b_mix, w_out=w_out, plane_offsets=plane_offsets, trainer_map=trainer_map)


gelu_c = 0.7978845608
gelu_k = 0.044715
visc = 0.1

def gelu_value(v):
    return 0.5 * v * (1.0 + jnp.tanh(gelu_c * (v + gelu_k * v * v * v)))

def gelu_slope(v):
    tval = jnp.tanh(gelu_c * (v + gelu_k * v * v * v))
    return 0.5 * (1.0 + tval) + 0.5 * v * (1.0 - tval * tval) * gelu_c * (1.0 + 3.0 * gelu_k * v * v)

def patches(plane, width_x, width_y):
    parts = [plane[:, a:a + width_x, b:b + width_y] for a in range(3) for b in range(3)]
    return jnp.stack(parts, axis=1).reshape(27, width_x * width_y)

def forward(pats, w_conv, b_conv, w_mix, b_mix, w_out):
    pre_one = lax.dot_general(pats, w_conv, (((0,), (0,)), ((), ())), preferred_element_type=jnp.float32) + b_conv
    hidden_one = gelu_value(pre_one).astype(jnp.bfloat16)
    pre_two = jnp.dot(hidden_one, w_mix, preferred_element_type=jnp.float32) + b_mix
    hidden_two = gelu_value(pre_two).astype(jnp.bfloat16)
    stress = lax.dot_general(w_out, hidden_two, (((0,), (1,)), ((), ())), preferred_element_type=jnp.float32)
    return (pre_one, hidden_one, pre_two, hidden_two, stress)

def train_grads(pats, target, scale, w_conv, b_conv, w_mix, b_mix, w_out):
    pre_one, hidden_one, pre_two, hidden_two, stress = forward(pats, w_conv, b_conv, w_mix, b_mix, w_out)
    errors = ((stress - target) * scale).astype(jnp.bfloat16)
    g_out = lax.dot_general(hidden_two, errors, (((0,), (1,)), ((), ())), preferred_element_type=jnp.float32)
    back_two = lax.dot_general(errors, w_out, (((0,), (1,)), ((), ())), preferred_element_type=jnp.float32)
    delta_two = (back_two * gelu_slope(pre_two)).astype(jnp.bfloat16)
    g_bmix = lax.optimization_barrier(jnp.sum(delta_two, axis=0, dtype=jnp.float32))
    g_mix = lax.dot_general(hidden_one, delta_two, (((0,), (0,)), ((), ())), preferred_element_type=jnp.float32)
    back_one = lax.dot_general(delta_two, w_mix, (((1,), (1,)), ((), ())), preferred_element_type=jnp.float32)
    delta_one = (back_one * gelu_slope(pre_one)).astype(jnp.bfloat16)
    g_bconv = lax.optimization_barrier(jnp.sum(delta_one, axis=0, dtype=jnp.float32))
    g_conv = lax.dot_general(pats, delta_one, (((1,), (0,)), ((), ())), preferred_element_type=jnp.float32)
    return (g_conv, g_bconv, g_mix, g_bmix, g_out)

def central(field, axis):
    return 0.5 * (jnp.roll(field, -1, axis) - jnp.roll(field, 1, axis))

def reference(velocity, target_stress, w_conv, b_conv, w_mix, b_mix, w_out, plane_offsets, trainer_map):
    weights = (w_conv, b_conv, w_mix, b_mix, w_out)
    vel_b = velocity.astype(jnp.bfloat16)

    def infer(plane):
        padded = jnp.pad(plane, ((0, 0), (1, 1), (1, 1)), mode='wrap')
        return forward(patches(padded, NX, NY), *weights)[4].reshape(6, NX, NY)
    stress = jnp.transpose(lax.map(infer, jnp.transpose(vel_b, (1, 0, 2, 3))), (1, 0, 2, 3))
    comps = []
    for comp in range(3):
        field = velocity[comp]
        lap = -6.0 * field
        for axis in range(3):
            lap = lap + jnp.roll(field, 1, axis) + jnp.roll(field, -1, axis)
        comps.append(lap)
    sxx, syy, szz, sxy, sxz, syz = [stress[c] for c in range(6)]
    force_x = central(sxx, 1) + central(sxy, 2) + central(sxz, 0)
    force_y = central(sxy, 1) + central(syy, 2) + central(syz, 0)
    force_z = central(sxz, 1) + central(syz, 2) + central(szz, 0)
    tendency = jnp.stack([visc * comps[0] - force_x, visc * comps[1] - force_y, visc * comps[2] - force_z])
    gscale = 1.0 / math.sqrt(SAMPLES * CX * CY)

    def one_sample(carry, index):
        g_idx = index // (N_SX * N_SY * S)
        i_idx = index // (N_SY * S) % N_SX
        j_idx = index // S % N_SY
        s_idx = index % S
        row = trainer_map[g_idx, i_idx, :, 0]
        dest = row[j_idx * S + s_idx]
        count = jnp.sum((row == dest).astype(jnp.float32))
        scale = 2.0 * gscale / count
        zero = jnp.zeros((), jnp.int32)
        plane_z = (g_idx * PZ + plane_offsets[g_idx, i_idx, j_idx, s_idx]).astype(jnp.int32)
        start_x = (i_idx * CX).astype(jnp.int32)
        start_y = (j_idx * CY).astype(jnp.int32)
        plane = lax.dynamic_slice(vel_b, (zero, plane_z, start_x, start_y), (3, 1, CX, CY))[:, 0]
        target = lax.dynamic_slice(target_stress, (zero, plane_z, start_x, start_y), (6, 1, CX, CY))[:, 0]
        padded = jnp.pad(plane, ((0, 0), (1, 1), (1, 1)))
        grads = train_grads(patches(padded, CX, CY), target.reshape(6, CX * CY), scale, *weights)
        return (tuple((a + b for a, b in zip(carry, grads))), None)
    start = (jnp.zeros((27, FEAT), jnp.float32), jnp.zeros((FEAT,), jnp.float32), jnp.zeros((FEAT, FEAT), jnp.float32), jnp.zeros((FEAT,), jnp.float32), jnp.zeros((FEAT, 6), jnp.float32))
    grads, _ = lax.scan(one_sample, start, jnp.arange(SAMPLES, dtype=jnp.int32))
    return (tendency, grads[0], grads[1], grads[2], grads[3], grads[4])
```

```python
import functools
import math

import jax
import jax.numpy as jnp
from jax import lax
from jax.experimental import pallas as pl
from jax.experimental.pallas import tpu as pltpu
from jax.sharding import PartitionSpec as P

f32 = jnp.float32
bf16 = jnp.bfloat16
MESH = pl.DeviceIdType.MESH
HIGH = lax.Precision.HIGHEST

S = 2
gelu_c = 0.7978845608
gelu_k = 0.044715
visc = 0.1
lam = (gelu_c * gelu_k) ** (1.0 / 3.0)
shift_c = gelu_c / lam

PZ = 8
CX = 32
CY = 128
BLK = 16
PLANE = (CX + 2) * BLK
TROW = 8
TPLANE = (CX + 2) * TROW
XC = 16
NC = XC * CY
GROWS = 192

DX = (0, 3, 4)
DY = (3, 1, 5)
DZ = (4, 5, 2)


def dot(a, b, precision=None):
    return jnp.dot(a, b, preferred_element_type=f32, precision=precision)


def dot_nt(a, b, precision=None):
    return lax.dot_general(
        a, b, (((1,), (1,)), ((), ())), preferred_element_type=f32, precision=precision
    )


def split(value):
    high = value.astype(bf16).astype(f32)
    return high, value - high


def gate(m):
    return (m * jnp.tanh(m * (m * m + shift_c))).astype(bf16)


def lanes(shape):
    return lax.broadcasted_iota(jnp.int32, shape, 1)


def rows(shape):
    return lax.broadcasted_iota(jnp.int32, shape, 0)


def load_patches(buffer, base, count):
    return jnp.concatenate(
        [
            buffer[pl.ds(pl.multiple_of(base + x * BLK, BLK), 3 * BLK), :]
            for x in range(count)
        ],
        axis=1,
    )


def kernel(
    n_sx, n_sy, n_grp, gscale,
    vel, tgt, wc, bc, wm, bm, wo, offs, tmap,
    tend, gconv, gbconv, gmix, gbmix, gout,
    qf, qb, sf, sb, tg, stress, cw, mw, ow, tw1, tw2, wb2, wbo, prep, prep2,
    q1, q2, lin, grad,
    rowsrc, rowdst, colsrc, coldst, zsrc, zdst, hr, cc,
    srowsrc, srowdst, scolsrc, scoldst, scc,
    gseg, ra, sb_sum, rb, fin, rc,
    hs, hrv, ss, srv, a_s, a_r, b_s, b_r, c_s, c_r,
):
    isx, isy, igr = lax.axis_index("sx"), lax.axis_index("sy"), lax.axis_index("grp")
    up_x, down_x = lax.rem(isx + 1, n_sx), lax.rem(isx + n_sx - 1, n_sx)
    ys = (lax.rem(isy + n_sy - 1, n_sy), isy, lax.rem(isy + 1, n_sy))
    other = 1 - igr
    n_b = n_sx * n_grp
    ib = isx * n_grp + igr

    barrier = pltpu.get_barrier_semaphore()

    def greet(device):
        pl.semaphore_signal(barrier, inc=1, device_id=device, device_id_type=MESH)

    def greet_sy(k, _):
        greet((isx, lax.rem(isy + k, n_sy), igr))
        return 0

    def greet_b(k, _):
        at = lax.rem(ib + k, n_b)
        greet((at // n_grp, isy, lax.rem(at, n_grp)))
        return 0

    lax.fori_loop(1, n_sy, greet_sy, 0)
    lax.fori_loop(1, n_b, greet_b, 0)
    for to_x in (up_x, down_x):
        for to_y in (ys[0], ys[2]):
            greet((to_x, to_y, igr))

    for c in range(3):
        for side, x in ((0, 0), (1, CX - 1)):
            rowsrc[side, 8 * c : 8 * c + 8, :] = vel[pl.ds(c * PZ * CX + x, PZ, stride=CX), :]
        for side, p in ((0, PZ - 1), (1, 0)):
            zsrc[side, c * CX : (c + 1) * CX, :] = vel[pl.ds((c * PZ + p) * CX, CX), :]
    lane = lanes((CX, CY))

    def pack_cols(p, acc):
        for c in range(3):
            j = c * PZ + p
            v = vel[pl.ds(pl.multiple_of(j * CX, CX), CX), :]
            acc = jnp.where(lane // 2 == j, pltpu.roll(v, 2 * j + 1, 1), acc)
        return acc

    colsrc[...] = lax.fori_loop(0, PZ, pack_cols, jnp.zeros((CX, CY), f32))

    pl.semaphore_wait(barrier, (n_sy - 1) + (n_b - 1) + 4)

    def halo_copies():
        out = []
        for d in (-1, 0, 1):
            for side, to_x in ((0, up_x), (1, down_x)):
                slot = 1 - d
                out.append(
                    pltpu.make_async_remote_copy(
                        src_ref=rowsrc.at[1 - side],
                        dst_ref=rowdst.at[side, slot],
                        send_sem=hs.at[side * 3 + slot],
                        recv_sem=hrv.at[side * 3 + slot],
                        device_id=(to_x, ys[1 + d], igr),
                        device_id_type=MESH,
                    )
                )
        for side, to_y in ((0, ys[2]), (1, ys[0])):
            out.append(
                pltpu.make_async_remote_copy(
                    src_ref=colsrc,
                    dst_ref=coldst.at[side],
                    send_sem=hs.at[6 + side],
                    recv_sem=hrv.at[6 + side],
                    device_id=(isx, to_y, igr),
                    device_id_type=MESH,
                )
            )
        for side in (0, 1):
            out.append(
                pltpu.make_async_remote_copy(
                    src_ref=zsrc.at[side],
                    dst_ref=zdst.at[side],
                    send_sem=hs.at[8 + side],
                    recv_sem=hrv.at[8 + side],
                    device_id=(isx, isy, other),
                    device_id_type=MESH,
                )
            )
        return out

    halo = halo_copies()
    for copy in halo:
        copy.start()

    prep[...] = jnp.zeros(prep.shape, f32)
    for c in range(3):
        for a in range(3):
            prep[a * BLK + c * 3 : a * BLK + c * 3 + 3, :] = wc[
                c * 9 + 3 * a : c * 9 + 3 * a + 3, :
            ].astype(f32)
    prep[9:10, :] = bc[...]
    w1 = prep[...][0:48, :]
    w2h = wm[...].astype(f32) * 0.5
    row48 = rows((48, 128))
    high, low = split(w1 * lam)
    pad = jnp.zeros((32, 128), f32)
    cw[...] = jnp.concatenate([high, low, pad], axis=0).T.astype(bf16)
    comp = dot(w1 * lam, w2h, HIGH)
    comp = comp + jnp.where(row48 == 9, lam * bm[...], 0.0)
    comp_high, comp_low = split(comp)
    pick16 = (
        (lanes((6, 16)) == rows((6, 16))) | (lanes((6, 16)) == rows((6, 16)) + 8)
    ).astype(bf16)
    wo16 = dot(wo[...], pick16)
    outl = dot(jnp.concatenate([w2h, comp], axis=0), wo16, HIGH)
    out_high, out_low = split(outl)
    outl = jnp.where(lanes((176, 16)) < 8, out_high, out_low)
    mw[0:128, 0:128] = w2h.T.astype(bf16)
    tail = jnp.concatenate([comp_high, comp_low, pad], axis=0)
    mw[0:128, 128:256] = tail.T.astype(bf16)
    prep2[...] = jnp.zeros(prep2.shape, f32)
    prep2[0:176, 0:16] = outl
    mw[128:144, 0:128] = prep2[0:128, :].T[0:16, :].astype(bf16)
    mw[128:144, 128:256] = prep2[128:256, :].T[0:16, :].astype(bf16)
    pick = (lanes((16, 6)) == rows((16, 6))).astype(bf16)
    ow[...] = dot_nt(pick, wo[...]).astype(bf16)
    half_b1 = 0.5 * bc[...]
    bh, rest = split(half_b1)
    bmid, rest = split(rest)
    t1 = jnp.where(row48 == 9, bh, jnp.where(row48 == 10, bmid, jnp.where(row48 == 11, rest, 0.5 * w1)))
    tw1[...] = jnp.concatenate([t1, pad, pad, pad[0:16]], axis=0).T.astype(bf16)
    half_b2 = 0.5 * bm[...]
    bh, rest = split(half_b2)
    bmid, rest = split(rest)
    row128 = rows((128, 128))
    t2 = jnp.where(row128 == 9, bh, jnp.where(row128 == 10, bmid, jnp.where(row128 == 11, rest, 0.0)))
    tw2[:, 0:128] = w2h.T.astype(bf16)
    tw2[:, 128:256] = t2.T.astype(bf16)
    wb2[...] = w2h.astype(bf16)
    wbo[...] = (0.5 * jnp.where(lanes((128, 16)) < 8, wo16, 0.0)).astype(bf16)

    sf[...] = jnp.ones(sf.shape, f32)
    zero8 = jnp.zeros((8, 128), f32)
    tg[...] = jnp.zeros(tg.shape, f32)
    for s in range(S):
        chosen = lax.broadcasted_iota(jnp.int32, (PZ, CX, CY), 0) == offs[s]

        def plane(ref, c, chosen=chosen):
            stack = ref[c * PZ * CX : (c + 1) * PZ * CX, :].reshape(PZ, CX, CY)
            return jnp.sum(jnp.where(chosen, stack, 0.0), axis=0)

        for side in (0, CX + 1):
            at = s * PLANE + side * BLK
            sf[at : at + 8, :] = zero8
            sf[at + 8 : at + 9, :] = zero8[0:1]
        for c in range(3):
            v = plane(vel, c)
            for b in range(3):
                if b == 0:
                    w = jnp.where(lane == 0, 0.0, pltpu.roll(v, 1, 1))
                elif b == 2:
                    w = jnp.where(lane == CY - 1, 0.0, pltpu.roll(v, CY - 1, 1))
                else:
                    w = v
                sf[pl.ds(s * PLANE + BLK + c * 3 + b, CX, stride=BLK), :] = w
        for c in range(6):
            tg[pl.ds(s * CX * TROW + c, CX, stride=TROW), :] = plane(tgt, c)
    sb[...] = sf[...].astype(bf16)
    grad[...] = jnp.zeros(grad.shape, f32)

    names = tmap[...]
    place = lanes(names.shape)

    def scale_of(s):
        dest = jnp.sum(jnp.where(place == isy * S + s, names, 0), axis=1, keepdims=True)
        count = jnp.sum((names == dest).astype(f32), axis=1, keepdims=True)
        return jnp.broadcast_to(2.0 * gscale / count, (8, 128))

    scales = [scale_of(s) for s in range(S)]

    def train(i, _):
        s = i // (CX // XC)
        part = lax.rem(i, CX // XC)
        scale = jnp.where(s == 0, scales[0], scales[1])
        pats = load_patches(sb, s * PLANE + part * (XC * BLK), XC)
        a1 = dot(tw1[:, 0:48], pats)
        p1 = (8.0 * gelu_c * gelu_k) * (a1 * a1) + 2.0 * gelu_c
        t1 = jnp.tanh(a1 * p1)
        s1 = 1.0 + t1
        h1 = (a1 * s1).astype(bf16)
        d1 = s1 * (1.0 + (1.0 - t1) * (a1 * (3.0 * p1 - 4.0 * gelu_c)))
        h1x = jnp.concatenate([h1, pats[0:16]], axis=0)
        a2 = dot(tw2[:, 0:144], h1x)
        p2 = (8.0 * gelu_c * gelu_k) * (a2 * a2) + 2.0 * gelu_c
        t2 = jnp.tanh(a2 * p2)
        s2 = 1.0 + t2
        h2 = (a2 * s2).astype(bf16)
        d2 = s2 * (1.0 + (1.0 - t2) * (a2 * (3.0 * p2 - 4.0 * gelu_c)))
        tau = dot(ow[...], h2)[0:8]
        tbase = s * (CX * TROW) + part * (XC * TROW)
        err = jnp.concatenate(
            [
                (
                    tau[:, x * CY : (x + 1) * CY]
                    - tg[pl.ds(pl.multiple_of(tbase + x * TROW, TROW), TROW), :]
                )
                * scale
                for x in range(XC)
            ],
            axis=1,
        )
        err = jnp.concatenate([err, jnp.zeros((8, NC), f32)], axis=0).astype(bf16)
        g2 = (dot(wbo[...], err) * d2).astype(bf16)
        g1 = (dot(wb2[...], g2) * d1).astype(bf16)
        grad[176:184, :] += dot_nt(err, h2)[0:8]
        mix = dot_nt(h1x, g2)
        grad[0:128, :] += mix[0:128]
        grad[184:192, :] += mix[136:144]
        grad[128:176, :] += dot_nt(pats, g1)
        return 0

    lax.fori_loop(0, S * CX // XC, train, 0)

    seg = GROWS // n_sy
    for j in range(n_sy):
        gseg[j] = grad[j * seg : (j + 1) * seg, :]

    def a_copy(k):
        to = lax.rem(isy + k, n_sy)
        return pltpu.make_async_remote_copy(
            src_ref=gseg.at[to], dst_ref=ra.at[isy],
            send_sem=a_s.at[to], recv_sem=a_r.at[isy],
            device_id=(isx, to, igr), device_id_type=MESH,
        )

    def a_arrival(k):
        of = lax.rem(isy + k, n_sy)
        return pltpu.make_async_remote_copy(
            src_ref=gseg.at[of], dst_ref=ra.at[of],
            send_sem=a_s.at[of], recv_sem=a_r.at[of],
            device_id=(isx, of, igr), device_id_type=MESH,
        )

    def b_copy(k, mine):
        at = lax.rem(ib + k, n_b)
        of = ib if mine else at
        return pltpu.make_async_remote_copy(
            src_ref=sb_sum, dst_ref=rb.at[of],
            send_sem=b_s.at[at], recv_sem=b_r.at[of],
            device_id=(at // n_grp, isy, lax.rem(at, n_grp)), device_id_type=MESH,
        )

    def c_copy(k, mine):
        at = lax.rem(isy + k, n_sy)
        of = isy if mine else at
        return pltpu.make_async_remote_copy(
            src_ref=fin, dst_ref=rc.at[of],
            send_sem=c_s.at[at], recv_sem=c_r.at[of],
            device_id=(isx, at, igr), device_id_type=MESH,
        )

    def each(count, act):
        def step(k, _):
            act(k)
            return 0

        lax.fori_loop(1, count, step, 0)

    ra[isy] = gseg[isy]
    each(n_sy, lambda k: a_copy(k).start())

    def second():
        each(n_sy, lambda k: a_arrival(k).wait_recv())
        total = ra[0]
        for j in range(1, n_sy):
            total = total + ra[j]
        sb_sum[...] = total
        rb[ib] = total
        each(n_b, lambda k: b_copy(k, True).start())

    def third():
        each(n_b, lambda k: b_copy(k, False).wait_recv())
        total = rb[0]
        for j in range(1, n_b):
            total = total + rb[j]
        fin[...] = total
        rc[isy] = total
        each(n_sy, lambda k: c_copy(k, True).start())

    qf[...] = jnp.ones(qf.shape, f32)
    for copy in halo[0:8]:
        copy.wait_recv()
    lane24 = lanes((24, CY))
    for side in (0, 1):
        left, mid, right = rowdst[side, 0], rowdst[side, 1], rowdst[side, 2]
        shifted = (
            jnp.where(lane24 == 0, pltpu.roll(left, 1, 1), pltpu.roll(mid, 1, 1)),
            mid,
            jnp.where(
                lane24 == CY - 1, pltpu.roll(right, CY - 1, 1), pltpu.roll(mid, CY - 1, 1)
            ),
        )
        at = side * (CX + 1) * BLK
        for b in range(3):
            hr[...] = shifted[b]
            for c in range(3):
                qf[pl.ds(at + c * 3 + b, PZ, stride=PLANE), :] = hr[8 * c : 8 * c + 8, :]
    cc[...] = jnp.where(
        lax.rem(lane, 2) == 0, pltpu.roll(coldst[1], CY - 1, 1), pltpu.roll(coldst[0], 1, 1)
    )

    def build(p, _):
        for c in range(3):
            j = c * PZ + p
            v = vel[pl.ds(pl.multiple_of(j * CX, CX), CX), :]
            edge = pltpu.roll(cc[...], CY - 1 - 2 * j, 1)
            at = p * PLANE + BLK + c * 3
            qf[pl.ds(at, CX, stride=BLK), :] = jnp.where(lane == 0, edge, pltpu.roll(v, 1, 1))
            qf[pl.ds(at + 1, CX, stride=BLK), :] = v
            qf[pl.ds(at + 2, CX, stride=BLK), :] = jnp.where(
                lane == CY - 1, edge, pltpu.roll(v, CY - 1, 1)
            )
        base = pl.ds(pl.multiple_of(p * PLANE, BLK), PLANE)
        qb[base, :] = qf[base, :].astype(bf16)
        return 0

    lax.fori_loop(0, PZ, build, 0)

    per = CX // XC
    chunks = PZ * per

    def where_is(i):
        turn = i // per
        p = jnp.where(turn == 0, 0, jnp.where(turn == 1, PZ - 1, turn - 1))
        return p, lax.rem(i, per)

    def patches_of(i):
        p, part = where_is(i)
        return load_patches(qb, p * PLANE + part * (XC * BLK), XC)

    def stage_conv(i):
        pats = patches_of(i)
        q1[...] = gate(dot(cw[:, 0:96], jnp.concatenate([pats, pats], axis=0)))

    def stage_mix(i):
        pats = patches_of(i)
        m2 = dot(mw[:, 0:224], jnp.concatenate([q1[...], pats, pats], axis=0))
        q2[...] = gate(m2[0:128])
        lin[...] = m2[128:136] + m2[136:144]

    def stage_out(i):
        p, part = where_is(i)
        tau = dot(ow[...], q2[...])[0:8] + lin[...]
        at = (p + 1) * TPLANE + (part * XC + 1) * TROW
        for x in range(XC):
            stress[pl.ds(pl.multiple_of(at + x * TROW, TROW), TROW), :] = tau[
                :, x * CY : (x + 1) * CY
            ]

    def z_copies():
        out = []
        for side, p in ((0, PZ), (1, 1)):
            out.append(
                pltpu.make_async_remote_copy(
                    src_ref=stress.at[pl.ds(p * TPLANE + TROW, CX * TROW)],
                    dst_ref=stress.at[pl.ds((PZ + 1) * side * TPLANE + TROW, CX * TROW)],
                    send_sem=ss.at[side],
                    recv_sem=srv.at[side],
                    device_id=(isx, isy, other),
                    device_id_type=MESH,
                )
            )
        return out

    zs = z_copies()

    def infer(i, _):
        stage_out(jnp.clip(i - 2, 0, chunks - 1))
        stage_mix(jnp.clip(i - 1, 0, chunks - 1))
        stage_conv(jnp.minimum(i, chunks - 1))

        @pl.when(i == 2 * per + 1)
        def _():
            for copy in zs:
                copy.start()

        @pl.when(i == 8)
        def _():
            second()

        @pl.when(i == 13)
        def _():
            third()

        return 0

    q1[...] = jnp.zeros(q1.shape, bf16)
    q2[...] = jnp.zeros(q2.shape, bf16)
    lin[...] = jnp.zeros(lin.shape, f32)
    lax.fori_loop(0, chunks + 2, infer, 0)

    for c in range(3):
        for side, x in ((0, 1), (1, CX)):
            srowsrc[side, 8 * c : 8 * c + 8, :] = stress[
                pl.ds(TPLANE + x * TROW + DX[c], PZ, stride=TPLANE), :
            ]

    def pack_stress(p, acc):
        for c in range(3):
            j = c * PZ + p
            v = stress[pl.ds((p + 1) * TPLANE + TROW + DY[c], CX, stride=TROW), :]
            acc = jnp.where(lane // 2 == j, pltpu.roll(v, 2 * j + 1, 1), acc)
        return acc

    scolsrc[...] = lax.fori_loop(0, PZ, pack_stress, jnp.zeros((CX, CY), f32))
    edges = []
    for side, to_x in ((0, up_x), (1, down_x)):
        edges.append(
            pltpu.make_async_remote_copy(
                src_ref=srowsrc.at[1 - side],
                dst_ref=srowdst.at[side],
                send_sem=ss.at[2 + side],
                recv_sem=srv.at[2 + side],
                device_id=(to_x, isy, igr),
                device_id_type=MESH,
            )
        )
    for side, to_y in ((0, ys[2]), (1, ys[0])):
        edges.append(
            pltpu.make_async_remote_copy(
                src_ref=scolsrc,
                dst_ref=scoldst.at[side],
                send_sem=ss.at[4 + side],
                recv_sem=srv.at[4 + side],
                device_id=(isx, to_y, igr),
                device_id_type=MESH,
            )
        )
    for copy in edges:
        copy.start()

    for copy in halo[8:10]:
        copy.wait_recv()

    def viscous(p, below, above):
        for c in range(3):
            at = p * PLANE + BLK + c * 3

            def pick_at(start):
                return qf[pl.ds(start, CX, stride=BLK), :]

            mid = pick_at(at + 1)
            total = pick_at(at) + pick_at(at + 2)
            total = total + pick_at(at + 1 - BLK) + pick_at(at + 1 + BLK)
            total = total + below(c) + above(c) - 6.0 * mid
            tend[pl.ds(pl.multiple_of((c * PZ + p) * CX, CX), CX), :] = visc * total

    def plane_of(p):
        return lambda c: vel[pl.ds(pl.multiple_of((c * PZ + p) * CX, CX), CX), :]

    def ghost(side):
        return lambda c: zdst[side, c * CX : (c + 1) * CX, :]

    viscous(0, ghost(0), plane_of(1))

    def inner(p, _):
        viscous(p, plane_of(p - 1), plane_of(p + 1))
        return 0

    lax.fori_loop(1, PZ - 1, inner, 0)
    viscous(PZ - 1, plane_of(PZ - 2), ghost(1))

    each(n_sy, lambda k: c_copy(k, False).wait_recv())
    for j in range(n_sy):
        grad[j * seg : (j + 1) * seg, :] = rc[j]
    gmix[...] = grad[0:128, :]
    for c in range(3):
        for a in range(3):
            at = 128 + a * BLK + c * 3
            gconv[c * 9 + 3 * a : c * 9 + 3 * a + 3, :] = grad[at : at + 3, :]
    gbconv[...] = grad[137:138, :]
    gbmix[...] = grad[185:186, :]
    gout[...] = jnp.concatenate(
        [grad[176:184, :], jnp.zeros((120, 128), f32)], axis=0
    ).T[:, 0:6]

    for copy in zs:
        copy.wait_send()
    for copy in edges + zs:
        copy.wait_recv()
    for side in (0, 1):
        for c in range(3):
            stress[
                pl.ds(TPLANE + side * (CX + 1) * TROW + DX[c], PZ, stride=TPLANE), :
            ] = srowdst[side, 8 * c : 8 * c + 8, :]
    scc[...] = jnp.where(
        lax.rem(lane, 2) == 0, pltpu.roll(scoldst[1], CY - 1, 1), pltpu.roll(scoldst[0], 1, 1)
    )
    half = 0.25 / lam

    def diverge(p, _):
        for c in range(3):
            j = c * PZ + p

            def pick_at(plane, x, comp):
                return stress[pl.ds((p + plane) * TPLANE + x * TROW + comp, CX, stride=TROW), :]

            along_x = pick_at(1, 2, DX[c]) - pick_at(1, 0, DX[c])
            v = pick_at(1, 1, DY[c])
            edge = pltpu.roll(scc[...], CY - 1 - 2 * j, 1)
            along_y = jnp.where(lane == CY - 1, edge, pltpu.roll(v, CY - 1, 1)) - jnp.where(
                lane == 0, edge, pltpu.roll(v, 1, 1)
            )
            along_z = pick_at(2, 1, DZ[c]) - pick_at(0, 1, DZ[c])
            at = pl.ds(pl.multiple_of(j * CX, CX), CX)
            tend[at, :] = tend[at, :] - half * (along_x + along_y + along_z)
        return 0

    lax.fori_loop(0, PZ, diverge, 0)

    for copy in halo + edges:
        copy.wait_send()
    each(n_sy, lambda k: a_copy(k).wait_send())
    each(n_b, lambda k: b_copy(k, True).wait_send())
    each(n_sy, lambda k: c_copy(k, True).wait_send())


def shards(velocity, target_stress, w_conv, b_conv, w_mix, b_mix, w_out, plane_offsets, trainer_map):
    n_sx, n_sy, n_grp = (lax.axis_size(a) for a in ("sx", "sy", "grp"))
    n_b = n_sx * n_grp
    seg = GROWS // n_sy
    gscale = 1.0 / math.sqrt(S * n_sx * n_sy * n_grp * CX * CY)
    vmem = pl.BlockSpec(memory_space=pltpu.VMEM)
    smem = pl.BlockSpec(memory_space=pltpu.SMEM)

    def buf(*shape, dtype=f32):
        return pltpu.VMEM(shape, dtype)

    def sems(count):
        return pltpu.SemaphoreType.DMA((count,))

    outs = pl.pallas_call(
        functools.partial(kernel, n_sx, n_sy, n_grp, gscale),
        out_shape=[
            jax.ShapeDtypeStruct((3 * PZ * CX, CY), f32),
            jax.ShapeDtypeStruct((27, 128), f32),
            jax.ShapeDtypeStruct((1, 128), f32),
            jax.ShapeDtypeStruct((128, 128), f32),
            jax.ShapeDtypeStruct((1, 128), f32),
            jax.ShapeDtypeStruct((128, 6), f32),
        ],
        in_specs=[vmem] * 7 + [smem, vmem],
        out_specs=[vmem] * 6,
        scratch_shapes=[
            buf(PZ * PLANE, CY), buf(PZ * PLANE, CY, dtype=bf16),
            buf(S * PLANE, CY), buf(S * PLANE, CY, dtype=bf16),
            buf(S * CX * TROW, CY),
            buf((PZ + 2) * TPLANE, CY),
            buf(128, 128, dtype=bf16), buf(144, 256, dtype=bf16), buf(16, 128, dtype=bf16),
            buf(128, 128, dtype=bf16), buf(128, 256, dtype=bf16),
            buf(128, 128, dtype=bf16), buf(128, 16, dtype=bf16),
            buf(128, 128), buf(256, 128),
            buf(128, NC, dtype=bf16), buf(128, NC, dtype=bf16), buf(8, NC),
            buf(GROWS, 128),
            buf(2, 24, CY), buf(2, 3, 24, CY), buf(CX, CY), buf(2, CX, CY),
            buf(2, 3 * CX, CY), buf(2, 3 * CX, CY),
            buf(24, CY), buf(CX, CY),
            buf(2, 24, CY), buf(2, 24, CY), buf(CX, CY), buf(2, CX, CY), buf(CX, CY),
            buf(n_sy, seg, 128), buf(n_sy, seg, 128),
            buf(seg, 128), buf(n_b, seg, 128),
            buf(seg, 128), buf(n_sy, seg, 128),
            sems(10), sems(10), sems(6), sems(6),
            sems(n_sy), sems(n_sy), sems(n_b), sems(n_b), sems(n_sy), sems(n_sy),
        ],
        compiler_params=pltpu.CompilerParams(
            collective_id=0, has_side_effects=True, vmem_limit_bytes=40 * 2**20
        ),
    )(
        velocity.reshape(3 * PZ * CX, CY),
        target_stress.reshape(6 * PZ * CX, CY),
        w_conv,
        b_conv.reshape(1, 128),
        w_mix,
        b_mix.reshape(1, 128),
        w_out,
        plane_offsets.reshape(S),
        trainer_map.reshape(1, n_sy * S),
    )
    return (
        outs[0].reshape(3, PZ, CX, CY),
        outs[1],
        outs[2].reshape(128),
        outs[3],
        outs[4].reshape(128),
        outs[5],
    )


def solution(mesh):
    in_specs = (
        P(None, "grp", "sx", "sy"),
        P(None, "grp", "sx", "sy"),
        P(),
        P(),
        P(),
        P(),
        P(),
        P("grp", "sx", "sy", None),
        P("grp", "sx", None, None),
    )
    out_specs = (P(None, "grp", "sx", "sy"), P(), P(), P(), P(), P())
    return jax.shard_map(shards, mesh=mesh, in_specs=in_specs, out_specs=out_specs, check_vma=False)
```

```python
import functools
import math

import jax
import jax.numpy as jnp
from jax import lax
from jax.experimental import pallas as pl
from jax.experimental.pallas import tpu as pltpu
from jax.sharding import PartitionSpec as P

f32 = jnp.float32
bf16 = jnp.bfloat16
MESH = pl.DeviceIdType.MESH
HIGH = lax.Precision.HIGHEST

S = 2
gelu_c = 0.7978845608
gelu_k = 0.044715
visc = 0.1
lam = (gelu_c * gelu_k) ** (1.0 / 3.0)
shift_c = gelu_c / lam

PZ = 8
CX = 32
CY = 128
BLK = 16
PLANE = (CX + 2) * BLK
TROW = 8
TPLANE = (CX + 2) * TROW
XC = 16
NC = XC * CY
PER = CX // XC
ORDER = (0, 7, 1, 2, 3, 4, 5, 6)
EARLY = 6
GROWS = 192

DX = (0, 3, 4)
DY = (3, 1, 5)
DZ = (4, 5, 2)


def dot(a, b, precision=None):
    return jnp.dot(a, b, preferred_element_type=f32, precision=precision)


def dot_nt(a, b, precision=None):
    return lax.dot_general(
        a, b, (((1,), (1,)), ((), ())), preferred_element_type=f32, precision=precision
    )


def split(value):
    high = value.astype(bf16).astype(f32)
    return high, value - high


def gate(m):
    return (m * jnp.tanh(m * (m * m + shift_c))).astype(bf16)


def gate_and_slope(m):
    m = m.astype(bf16)
    z = m * (m * m + bf16(shift_c))
    t = jnp.tanh(z)
    up = bf16(1.0) + t
    down = bf16(1.0) - t
    return m * up, up * (bf16(1.0) + down * (bf16(3.0) * z - bf16(2.0 * shift_c) * m))


def lanes(shape):
    return lax.broadcasted_iota(jnp.int32, shape, 1)


def rows(shape):
    return lax.broadcasted_iota(jnp.int32, shape, 0)


def load_patches(buffer, base, count):
    return jnp.concatenate(
        [
            buffer[pl.ds(pl.multiple_of(base + x * BLK, BLK), 3 * BLK), :]
            for x in range(count)
        ],
        axis=1,
    )


def kernel(
    n_sx, n_sy, n_grp, gscale,
    vel_in, tgt_in, wc, bc, wm, bm, wo, offs, tmap,
    tend, gconv, gbconv, gmix, gbmix, gout,
    vel, tgt,
    qf, qb, sf, sb, tg, stress, cw, mw, ow, tw2, wb2, wbo, prep, prep2,
    q1, q2, lin, grad, h1, d1, h2, d2, g2,
    rowsrc, rowdst, colsrc, coldst, zsrc, zdst, hr, cc,
    srowsrc, srowdst, scolsrc, scoldst, scc,
    gseg, ra, sb_sum, rb, fin, rc,
    ins, hs, hrv, ss, srv, a_s, a_r, b_s, b_r, c_s, c_r,
):
    isx, isy, igr = lax.axis_index("sx"), lax.axis_index("sy"), lax.axis_index("grp")
    up_x, down_x = lax.rem(isx + 1, n_sx), lax.rem(isx + n_sx - 1, n_sx)
    ys = (lax.rem(isy + n_sy - 1, n_sy), isy, lax.rem(isy + 1, n_sy))
    other = 1 - igr
    n_b = n_sx * n_grp
    ib = isx * n_grp + igr

    loads = [
        pltpu.make_async_copy(vel_in, vel, ins.at[0]),
        pltpu.make_async_copy(tgt_in, tgt, ins.at[1]),
    ]
    for copy in loads:
        copy.start()

    barrier = pltpu.get_barrier_semaphore()

    def greet(device):
        pl.semaphore_signal(barrier, inc=1, device_id=device, device_id_type=MESH)

    def greet_sy(k, _):
        greet((isx, lax.rem(isy + k, n_sy), igr))
        return 0

    def greet_b(k, _):
        at = lax.rem(ib + k, n_b)
        greet((at // n_grp, isy, lax.rem(at, n_grp)))
        return 0

    lax.fori_loop(1, n_sy, greet_sy, 0)
    lax.fori_loop(1, n_b, greet_b, 0)
    for to_x in (up_x, down_x):
        for to_y in (ys[0], ys[2]):
            greet((to_x, to_y, igr))

    prep[...] = jnp.zeros(prep.shape, f32)
    for c in range(3):
        for a in range(3):
            prep[a * BLK + c * 3 : a * BLK + c * 3 + 3, :] = wc[
                c * 9 + 3 * a : c * 9 + 3 * a + 3, :
            ].astype(f32)
    prep[9:10, :] = bc[...]
    w1 = prep[...][0:48, :]
    w2h = wm[...].astype(f32) * 0.5
    row48 = rows((48, 128))
    high, low = split(w1 * lam)
    pad = jnp.zeros((32, 128), f32)
    cw[...] = jnp.concatenate([high, low, pad], axis=0).T.astype(bf16)
    comp = dot(w1 * lam, w2h, HIGH)
    comp = comp + jnp.where(row48 == 9, lam * bm[...], 0.0)
    comp_high, comp_low = split(comp)
    pick = (lanes((16, 6)) == rows((16, 6))) | (lanes((16, 6)) + 8 == rows((16, 6)))
    wo_rows = dot(pick.astype(bf16), wo[...])
    ow[...] = jnp.where(rows((16, 128)) < 8, wo_rows, 0.0).astype(bf16)
    prep[...] = jnp.zeros(prep.shape, f32)
    prep[0:16, :] = wo_rows
    wo16 = prep[...].T[:, 0:16]
    outl = dot(jnp.concatenate([w2h, comp], axis=0), wo16, HIGH)
    out_high, out_low = split(outl)
    outl = jnp.where(lanes((176, 16)) < 8, out_high, out_low)
    mw[0:128, 0:128] = w2h.T.astype(bf16)
    tail = jnp.concatenate([comp_high, comp_low, pad], axis=0)
    mw[0:128, 128:256] = tail.T.astype(bf16)
    prep2[...] = jnp.zeros(prep2.shape, f32)
    prep2[0:176, 0:16] = outl
    mw[128:144, 0:128] = prep2[0:128, :].T[0:16, :].astype(bf16)
    mw[128:144, 128:256] = prep2[128:256, :].T[0:16, :].astype(bf16)
    bh, rest = split(lam * bm[...])
    bmid, rest = split(rest)
    row128 = rows((128, 128))
    t2 = jnp.where(row128 == 9, bh, jnp.where(row128 == 10, bmid, jnp.where(row128 == 11, rest, 0.0)))
    tw2[:, 0:128] = w2h.T.astype(bf16)
    tw2[:, 128:256] = t2.T.astype(bf16)
    wb2[...] = w2h.astype(bf16)
    wbo[...] = (0.5 * jnp.where(lanes((128, 16)) < 8, wo16, 0.0)).astype(bf16)

    loads[0].wait()
    for c in range(3):
        for side, x in ((0, 0), (1, CX - 1)):
            rowsrc[side, 8 * c : 8 * c + 8, :] = vel[pl.ds(c * PZ * CX + x, PZ, stride=CX), :]
        for side, p in ((0, PZ - 1), (1, 0)):
            zsrc[side, c * CX : (c + 1) * CX, :] = vel[pl.ds((c * PZ + p) * CX, CX), :]
    lane = lanes((CX, CY))

    def pack_cols(p, acc):
        for c in range(3):
            j = c * PZ + p
            v = vel[pl.ds(pl.multiple_of(j * CX, CX), CX), :]
            acc = jnp.where(lane // 2 == j, pltpu.roll(v, 2 * j + 1, 1), acc)
        return acc

    colsrc[...] = lax.fori_loop(0, PZ, pack_cols, jnp.zeros((CX, CY), f32))

    def halo_copies():
        out = []
        for d in (-1, 0, 1):
            for side, to_x in ((0, up_x), (1, down_x)):
                slot = 1 - d
                out.append(
                    pltpu.make_async_remote_copy(
                        src_ref=rowsrc.at[1 - side],
                        dst_ref=rowdst.at[side, slot],
                        send_sem=hs.at[side * 3 + slot],
                        recv_sem=hrv.at[side * 3 + slot],
                        device_id=(to_x, ys[1 + d], igr),
                        device_id_type=MESH,
                    )
                )
        for side, to_y in ((0, ys[2]), (1, ys[0])):
            out.append(
                pltpu.make_async_remote_copy(
                    src_ref=colsrc,
                    dst_ref=coldst.at[side],
                    send_sem=hs.at[6 + side],
                    recv_sem=hrv.at[6 + side],
                    device_id=(isx, to_y, igr),
                    device_id_type=MESH,
                )
            )
        for side in (0, 1):
            out.append(
                pltpu.make_async_remote_copy(
                    src_ref=zsrc.at[side],
                    dst_ref=zdst.at[side],
                    send_sem=hs.at[8 + side],
                    recv_sem=hrv.at[8 + side],
                    device_id=(isx, isy, other),
                    device_id_type=MESH,
                )
            )
        return out

    halo = halo_copies()

    def enter():
        pl.semaphore_wait(barrier, (n_sy - 1) + (n_b - 1) + 4)
        for copy in halo:
            copy.start()

    loads[1].wait()
    names = tmap[...]
    place = lanes(names.shape)

    def scale_of(s):
        dest = jnp.sum(jnp.where(place == isy * S + s, names, 0), axis=1, keepdims=True)
        count = jnp.sum((names == dest).astype(f32), axis=1, keepdims=True)
        return 2.0 * gscale / count

    scales = [scale_of(s) for s in range(S)]

    sf[...] = jnp.ones(sf.shape, f32)
    zero8 = jnp.zeros((8, 128), f32)
    tg[...] = jnp.zeros(tg.shape, f32)
    for s in range(S):
        chosen = lax.broadcasted_iota(jnp.int32, (PZ, CX, CY), 0) == offs[s]

        def plane(ref, c, chosen=chosen):
            stack = ref[c * PZ * CX : (c + 1) * PZ * CX, :].reshape(PZ, CX, CY)
            return jnp.sum(jnp.where(chosen, stack, 0.0), axis=0)

        for side in (0, CX + 1):
            at = s * PLANE + side * BLK
            sf[at : at + 8, :] = zero8
            sf[at + 8 : at + 9, :] = zero8[0:1]
        for c in range(3):
            v = plane(vel, c)
            for b in range(3):
                if b == 0:
                    w = jnp.where(lane == 0, 0.0, pltpu.roll(v, 1, 1))
                elif b == 2:
                    w = jnp.where(lane == CY - 1, 0.0, pltpu.roll(v, CY - 1, 1))
                else:
                    w = v
                sf[pl.ds(s * PLANE + BLK + c * 3 + b, CX, stride=BLK), :] = w
        for c in range(6):
            tg[pl.ds(s * CX * TROW + c, CX, stride=TROW), :] = scales[s] * plane(tgt, c)
    sb[...] = sf[...].astype(bf16)
    grad[...] = jnp.zeros(grad.shape, f32)

    def sample_patches(k):
        s, part = k // PER, k % PER
        return load_patches(sb, s * PLANE + part * (XC * BLK), XC)

    def train_conv(k):
        pats = sample_patches(k)
        m = dot(cw[:, 0:96], jnp.concatenate([pats, pats], axis=0))
        h1[k], d1[k] = gate_and_slope(m)

    def train_mix(k):
        pats = sample_patches(k)
        h2[k], d2[k] = gate_and_slope(
            dot(tw2[:, 0:144], jnp.concatenate([h1[k], pats[0:16]], axis=0))
        )

    def train_out(k):
        s, part = k // PER, k % PER
        tau = dot(ow[...], h2[k])[0:8] * (scales[s] * (0.5 / lam))
        at = s * (CX * TROW) + part * (XC * TROW)
        target = jnp.concatenate(
            [tg[at + x * TROW : at + (x + 1) * TROW, :] for x in range(XC)], axis=1
        )
        err = jnp.concatenate([tau - target, jnp.zeros((8, NC), f32)], axis=0).astype(bf16)
        g2[k] = dot(wbo[...], err).astype(bf16) * d2[k]
        grad[176:184, :] += dot_nt(err, h2[k])[0:8]

    def train_back(k):
        pats = sample_patches(k)
        g1 = dot(wb2[...], g2[k]).astype(bf16) * d1[k]
        mix = dot_nt(jnp.concatenate([h1[k], pats[0:16]], axis=0), g2[k])
        grad[0:128, :] += mix[0:128]
        grad[184:192, :] += mix[136:144]
        grad[128:176, :] += dot_nt(pats, g1)

    parts = S * PER
    for k in range(parts + 3):
        if 0 <= k - 3:
            train_back(k - 3)
        if 0 <= k - 2 < parts:
            train_out(k - 2)
        if 0 <= k - 1 < parts:
            train_mix(k - 1)
        if k < parts:
            train_conv(k)
        if k == 2:
            enter()
    grad[0:128, :] = grad[0:128, :] * (0.5 / lam)
    grad[176:184, :] = grad[176:184, :] * (0.5 / lam)

    seg = GROWS // n_sy
    for j in range(n_sy):
        gseg[j] = grad[j * seg : (j + 1) * seg, :]

    def a_copy(k):
        to = lax.rem(isy + k, n_sy)
        return pltpu.make_async_remote_copy(
            src_ref=gseg.at[to], dst_ref=ra.at[isy],
            send_sem=a_s.at[to], recv_sem=a_r.at[isy],
            device_id=(isx, to, igr), device_id_type=MESH,
        )

    def a_arrival(k):
        of = lax.rem(isy + k, n_sy)
        return pltpu.make_async_remote_copy(
            src_ref=gseg.at[of], dst_ref=ra.at[of],
            send_sem=a_s.at[of], recv_sem=a_r.at[of],
            device_id=(isx, of, igr), device_id_type=MESH,
        )

    def b_copy(k, mine):
        at = lax.rem(ib + k, n_b)
        of = ib if mine else at
        return pltpu.make_async_remote_copy(
            src_ref=sb_sum, dst_ref=rb.at[of],
            send_sem=b_s.at[at], recv_sem=b_r.at[of],
            device_id=(at // n_grp, isy, lax.rem(at, n_grp)), device_id_type=MESH,
        )

    def c_copy(k, mine):
        at = lax.rem(isy + k, n_sy)
        of = isy if mine else at
        return pltpu.make_async_remote_copy(
            src_ref=fin, dst_ref=rc.at[of],
            send_sem=c_s.at[at], recv_sem=c_r.at[of],
            device_id=(isx, at, igr), device_id_type=MESH,
        )

    def each(count, act):
        def step(k, _):
            act(k)
            return 0

        lax.fori_loop(1, count, step, 0)

    ra[isy] = gseg[isy]
    each(n_sy, lambda k: a_copy(k).start())

    def second():
        each(n_sy, lambda k: a_arrival(k).wait_recv())
        total = ra[0]
        for j in range(1, n_sy):
            total = total + ra[j]
        sb_sum[...] = total
        rb[ib] = total
        each(n_b, lambda k: b_copy(k, True).start())

    def third():
        each(n_b, lambda k: b_copy(k, False).wait_recv())
        total = rb[0]
        for j in range(1, n_b):
            total = total + rb[j]
        fin[...] = total
        rc[isy] = total
        each(n_sy, lambda k: c_copy(k, True).start())

    qf[...] = jnp.ones(qf.shape, f32)
    for copy in halo[0:8]:
        copy.wait_recv()
    lane24 = lanes((24, CY))
    for side in (0, 1):
        left, mid, right = rowdst[side, 0], rowdst[side, 1], rowdst[side, 2]
        shifted = (
            jnp.where(lane24 == 0, pltpu.roll(left, 1, 1), pltpu.roll(mid, 1, 1)),
            mid,
            jnp.where(
                lane24 == CY - 1, pltpu.roll(right, CY - 1, 1), pltpu.roll(mid, CY - 1, 1)
            ),
        )
        at = side * (CX + 1) * BLK
        for b in range(3):
            hr[...] = shifted[b]
            for c in range(3):
                qf[pl.ds(at + c * 3 + b, PZ, stride=PLANE), :] = hr[8 * c : 8 * c + 8, :]
    cc[...] = jnp.where(
        lax.rem(lane, 2) == 0, pltpu.roll(coldst[1], CY - 1, 1), pltpu.roll(coldst[0], 1, 1)
    )

    def build(p):
        for c in range(3):
            j = c * PZ + p
            v = vel[pl.ds(pl.multiple_of(j * CX, CX), CX), :]
            edge = pltpu.roll(cc[...], CY - 1 - 2 * j, 1)
            at = p * PLANE + BLK + c * 3
            qf[pl.ds(at, CX, stride=BLK), :] = jnp.where(lane == 0, edge, pltpu.roll(v, 1, 1))
            qf[pl.ds(at + 1, CX, stride=BLK), :] = v
            qf[pl.ds(at + 2, CX, stride=BLK), :] = jnp.where(
                lane == CY - 1, edge, pltpu.roll(v, CY - 1, 1)
            )
        base = pl.ds(pl.multiple_of(p * PLANE, BLK), PLANE)
        qb[base, :] = qf[base, :].astype(bf16)

    def patches_of(k):
        return load_patches(qb, ORDER[k // PER] * PLANE + (k % PER) * (XC * BLK), XC)

    def stage_conv(k):
        pats = patches_of(k)
        q1[k % 2] = gate(dot(cw[:, 0:96], jnp.concatenate([pats, pats], axis=0)))

    def stage_mix(k):
        pats = patches_of(k)
        m2 = dot(mw[:, 0:224], jnp.concatenate([q1[k % 2], pats, pats], axis=0))
        q2[k % 2] = gate(m2[0:128])
        lin[k % 2] = m2[128:136] + m2[136:144]

    def stage_out(k):
        tau = dot(ow[...], q2[k % 2])[0:8] + lin[k % 2]
        at = (ORDER[k // PER] + 1) * TPLANE + (k % PER * XC + 1) * TROW
        for x in range(XC):
            stress[at + x * TROW : at + (x + 1) * TROW, :] = tau[:, x * CY : (x + 1) * CY]

    def z_copies():
        out = []
        for side, p in ((0, PZ), (1, 1)):
            out.append(
                pltpu.make_async_remote_copy(
                    src_ref=stress.at[pl.ds(p * TPLANE + TROW, CX * TROW)],
                    dst_ref=stress.at[pl.ds((PZ + 1) * side * TPLANE + TROW, CX * TROW)],
                    send_sem=ss.at[side],
                    recv_sem=srv.at[side],
                    device_id=(isx, isy, other),
                    device_id_type=MESH,
                )
            )
        return out

    zs = z_copies()

    scolsrc[...] = jnp.zeros(scolsrc.shape, f32)
    srowsrc[...] = jnp.zeros(srowsrc.shape, f32)

    def edge_copies(group):
        out = []
        for side, to_x in ((0, up_x), (1, down_x)):
            out.append(
                pltpu.make_async_remote_copy(
                    src_ref=srowsrc.at[group, 1 - side],
                    dst_ref=srowdst.at[group, side],
                    send_sem=ss.at[2 + 4 * group + side],
                    recv_sem=srv.at[2 + 4 * group + side],
                    device_id=(to_x, isy, igr),
                    device_id_type=MESH,
                )
            )
        for side, to_y in ((0, ys[2]), (1, ys[0])):
            out.append(
                pltpu.make_async_remote_copy(
                    src_ref=scolsrc.at[group],
                    dst_ref=scoldst.at[group, side],
                    send_sem=ss.at[4 + 4 * group + side],
                    recv_sem=srv.at[4 + 4 * group + side],
                    device_id=(isx, to_y, igr),
                    device_id_type=MESH,
                )
            )
        return out

    edges = [edge_copies(0), edge_copies(1)]
    groups = (ORDER[:EARLY], ORDER[EARLY:])

    def send_edges(group):
        acc = jnp.zeros((CX, CY), f32)
        for p in groups[group]:
            for c in range(3):
                j = c * PZ + p
                at = (p + 1) * TPLANE
                for side, x in ((0, 1), (1, CX)):
                    srowsrc[group, side, j : j + 1, :] = stress[
                        at + x * TROW + DX[c] : at + x * TROW + DX[c] + 1, :
                    ]
                v = stress[pl.ds(at + TROW + DY[c], CX, stride=TROW), :]
                acc = jnp.where(lane // 2 == j, pltpu.roll(v, 2 * j + 1, 1), acc)
        scolsrc[group] = acc
        for copy in edges[group]:
            copy.start()

    chunks = PZ * PER
    build(ORDER[0])
    for k in range(chunks + 2):
        if k % PER == 0 and k // PER + 1 < PZ:
            build(ORDER[k // PER + 1])
        if 0 <= k - 2:
            stage_out(k - 2)
        if 0 <= k - 1 < chunks:
            stage_mix(k - 1)
        if k < chunks:
            stage_conv(k)
        if k - 2 == 2 * PER - 1:
            for copy in zs:
                copy.start()
        if k - 2 == EARLY * PER - 1:
            send_edges(0)
        if k == 8:
            second()
        if k == 14:
            third()
    send_edges(1)

    for copy in halo[8:10]:
        copy.wait_recv()

    def viscous(p, below, above):
        for c in range(3):
            at = p * PLANE + BLK + c * 3

            def pick_at(start):
                return qf[pl.ds(start, CX, stride=BLK), :]

            mid = pick_at(at + 1)
            total = pick_at(at) + pick_at(at + 2)
            total = total + pick_at(at + 1 - BLK) + pick_at(at + 1 + BLK)
            total = total + below(c) + above(c) - 6.0 * mid
            tend[pl.ds(pl.multiple_of((c * PZ + p) * CX, CX), CX), :] = visc * total

    def plane_of(p):
        return lambda c: vel[pl.ds(pl.multiple_of((c * PZ + p) * CX, CX), CX), :]

    def ghost(side):
        return lambda c: zdst[side, c * CX : (c + 1) * CX, :]

    viscous(0, ghost(0), plane_of(1))

    def inner(p, _):
        viscous(p, plane_of(p - 1), plane_of(p + 1))
        return 0

    lax.fori_loop(1, PZ - 1, inner, 0)
    viscous(PZ - 1, plane_of(PZ - 2), ghost(1))

    each(n_sy, lambda k: c_copy(k, False).wait_recv())
    for j in range(n_sy):
        grad[j * seg : (j + 1) * seg, :] = rc[j]
    gmix[...] = grad[0:128, :]
    for c in range(3):
        for a in range(3):
            at = 128 + a * BLK + c * 3
            gconv[c * 9 + 3 * a : c * 9 + 3 * a + 3, :] = grad[at : at + 3, :]
    gbconv[...] = grad[137:138, :]
    gbmix[...] = grad[185:186, :]
    gout[...] = grad[176:182, :]

    half = 0.25 / lam

    def diverge(p):
        for c in range(3):
            j = c * PZ + p

            def pick_at(plane, x, comp):
                return stress[pl.ds((p + plane) * TPLANE + x * TROW + comp, CX, stride=TROW), :]

            along_x = pick_at(1, 2, DX[c]) - pick_at(1, 0, DX[c])
            v = pick_at(1, 1, DY[c])
            edge = pltpu.roll(scc[...], CY - 1 - 2 * j, 1)
            along_y = jnp.where(lane == CY - 1, edge, pltpu.roll(v, CY - 1, 1)) - jnp.where(
                lane == 0, edge, pltpu.roll(v, 1, 1)
            )
            along_z = pick_at(2, 1, DZ[c]) - pick_at(0, 1, DZ[c])
            at = pl.ds(j * CX, CX)
            tend[at, :] = tend[at, :] - half * (along_x + along_y + along_z)

    for copy in zs:
        copy.wait_send()
        copy.wait_recv()
    for group in (0, 1):
        for copy in edges[group]:
            copy.wait_recv()
        for p in groups[group]:
            for side in (0, 1):
                for c in range(3):
                    at = (p + 1) * TPLANE + side * (CX + 1) * TROW + DX[c]
                    stress[at : at + 1, :] = srowdst[group, side, c * PZ + p : c * PZ + p + 1, :]
        scc[...] = jnp.where(
            lax.rem(lane, 2) == 0,
            pltpu.roll(scoldst[group, 1], CY - 1, 1),
            pltpu.roll(scoldst[group, 0], 1, 1),
        )
        for p in groups[group]:
            diverge(p)

    for copy in halo + edges[0] + edges[1]:
        copy.wait_send()
    each(n_sy, lambda k: a_copy(k).wait_send())
    each(n_b, lambda k: b_copy(k, True).wait_send())
    each(n_sy, lambda k: c_copy(k, True).wait_send())


def write_out(*refs):
    for source, result in zip(refs[:6], refs[6:]):
        result[...] = source[...]


def shards(velocity, target_stress, w_conv, b_conv, w_mix, b_mix, w_out, plane_offsets, trainer_map):
    n_sx, n_sy, n_grp = (lax.axis_size(a) for a in ("sx", "sy", "grp"))
    n_b = n_sx * n_grp
    seg = GROWS // n_sy
    gscale = 1.0 / math.sqrt(S * n_sx * n_sy * n_grp * CX * CY)
    vmem = pl.BlockSpec(memory_space=pltpu.VMEM)
    smem = pl.BlockSpec(memory_space=pltpu.SMEM)
    hbm = pl.BlockSpec(memory_space=pltpu.HBM)

    def buf(*shape, dtype=f32):
        return pltpu.VMEM(shape, dtype)

    def sems(count):
        return pltpu.SemaphoreType.DMA((count,))

    outs = pl.pallas_call(
        functools.partial(kernel, n_sx, n_sy, n_grp, gscale),
        out_shape=[
            jax.ShapeDtypeStruct((3 * PZ * CX, CY), f32),
            jax.ShapeDtypeStruct((27, 128), f32),
            jax.ShapeDtypeStruct((1, 128), f32),
            jax.ShapeDtypeStruct((128, 128), f32),
            jax.ShapeDtypeStruct((1, 128), f32),
            jax.ShapeDtypeStruct((6, 128), f32),
        ],
        in_specs=[hbm] * 2 + [vmem] * 5 + [smem, vmem],
        out_specs=[vmem] * 6,
        scratch_shapes=[
            buf(3 * PZ * CX, CY), buf(6 * PZ * CX, CY),
            buf(PZ * PLANE, CY), buf(PZ * PLANE, CY, dtype=bf16),
            buf(S * PLANE, CY), buf(S * PLANE, CY, dtype=bf16),
            buf(S * CX * TROW, CY),
            buf((PZ + 2) * TPLANE, CY),
            buf(128, 128, dtype=bf16), buf(144, 256, dtype=bf16), buf(16, 128, dtype=bf16),
            buf(128, 256, dtype=bf16),
            buf(128, 128, dtype=bf16), buf(128, 16, dtype=bf16),
            buf(128, 128), buf(256, 128),
            buf(2, 128, NC, dtype=bf16), buf(2, 128, NC, dtype=bf16), buf(2, 8, NC),
            buf(GROWS, 128),
            *[buf(S * PER, 128, NC, dtype=bf16) for _ in range(5)],
            buf(2, 24, CY), buf(2, 3, 24, CY), buf(CX, CY), buf(2, CX, CY),
            buf(2, 3 * CX, CY), buf(2, 3 * CX, CY),
            buf(24, CY), buf(CX, CY),
            buf(2, 2, 24, CY), buf(2, 2, 24, CY), buf(2, CX, CY), buf(2, 2, CX, CY), buf(CX, CY),
            buf(n_sy, seg, 128), buf(n_sy, seg, 128),
            buf(seg, 128), buf(n_b, seg, 128),
            buf(seg, 128), buf(n_sy, seg, 128),
            sems(2), sems(10), sems(10), sems(10), sems(10),
            sems(n_sy), sems(n_sy), sems(n_b), sems(n_b), sems(n_sy), sems(n_sy),
        ],
        compiler_params=pltpu.CompilerParams(
            collective_id=0, has_side_effects=True, vmem_limit_bytes=62 * 2**20
        ),
    )(
        velocity.reshape(3 * PZ * CX, CY),
        target_stress.reshape(6 * PZ * CX, CY),
        w_conv,
        b_conv.reshape(1, 128),
        w_mix,
        b_mix.reshape(1, 128),
        w_out.T,
        plane_offsets.reshape(S),
        trainer_map.reshape(1, n_sy * S),
    )
    outs = pl.pallas_call(
        write_out,
        out_shape=[jax.ShapeDtypeStruct(o.shape, o.dtype) for o in outs],
        in_specs=[vmem] * 6,
        out_specs=[vmem] * 6,
    )(*outs)
    return (
        outs[0].reshape(3, PZ, CX, CY),
        outs[1],
        outs[2].reshape(128),
        outs[3],
        outs[4].reshape(128),
        outs[5].T,
    )


def solution(mesh):
    in_specs = (
        P(None, "grp", "sx", "sy"),
        P(None, "grp", "sx", "sy"),
        P(),
        P(),
        P(),
        P(),
        P(),
        P("grp", "sx", "sy", None),
        P("grp", "sx", None, None),
    )
    out_specs = (P(None, "grp", "sx", "sy"), P(), P(), P(), P(), P())
    return jax.shard_map(shards, mesh=mesh, in_specs=in_specs, out_specs=out_specs, check_vma=False)
```

```python
import functools
import math

import jax
import jax.numpy as jnp
from jax import lax
from jax.experimental import pallas as pl
from jax.experimental.pallas import tpu as pltpu
from jax.sharding import PartitionSpec as P

f32 = jnp.float32
bf16 = jnp.bfloat16
MESH = pl.DeviceIdType.MESH
HIGH = lax.Precision.HIGHEST

S = 2
gelu_c = 0.7978845608
gelu_k = 0.044715
visc = 0.1
lam = (gelu_c * gelu_k) ** (1.0 / 3.0)
shift_c = gelu_c / lam

PZ = 8
CX = 32
CY = 128
BLK = 16
PLANE = (CX + 2) * BLK
TROW = 8
TPLANE = (CX + 2) * TROW
XC = 16
NC = XC * CY
PER = CX // XC
ORDER = (0, 7, 1, 2, 3, 4, 5, 6)
EARLY = 6
GROWS = 192

DX = (0, 3, 4)
DY = (3, 1, 5)
DZ = (4, 5, 2)


def dot(a, b, precision=None):
    return jnp.dot(a, b, preferred_element_type=f32, precision=precision)


def dot_nt(a, b, precision=None):
    return lax.dot_general(
        a, b, (((1,), (1,)), ((), ())), preferred_element_type=f32, precision=precision
    )


def split(value):
    high = value.astype(bf16).astype(f32)
    return high, value - high


def gate(m):
    return (m * jnp.tanh(m * (m * m + shift_c))).astype(bf16)


def gate_and_slope(m):
    m = m.astype(bf16)
    z = m * (m * m + bf16(shift_c))
    t = jnp.tanh(z)
    up = bf16(1.0) + t
    down = bf16(1.0) - t
    return m * up, up * (bf16(1.0) + down * (bf16(3.0) * z - bf16(2.0 * shift_c) * m))


def lanes(shape):
    return lax.broadcasted_iota(jnp.int32, shape, 1)


def rows(shape):
    return lax.broadcasted_iota(jnp.int32, shape, 0)


def load_patches(buffer, base, count):
    return jnp.concatenate(
        [
            buffer[pl.ds(pl.multiple_of(base + x * BLK, BLK), 3 * BLK), :]
            for x in range(count)
        ],
        axis=1,
    )


def kernel(
    n_sx, n_sy, n_grp, gscale,
    vel_in, tgt_in, wc, bc, wm, bm, wo, offs, tmap,
    tend, gconv, gbconv, gmix, gbmix, gout,
    vel, tgt,
    qf, qb, sf, sb, tg, stress, cw, mw, ow, tw2, wb2, wbo, prep, prep2,
    q1, q2, lin, grad, h1, d1, h2, d2, g2,
    rowsrc, colsrc, hdst, zsrc, zdst, hr, cc,
    srowsrc, scolsrc, edst, scc,
    ra, part_a, rb, part_b, rc, part_c, rd,
    ins, hs, hrv, ss, srv, rs, rr,
):
    isx, isy, igr = lax.axis_index("sx"), lax.axis_index("sy"), lax.axis_index("grp")
    up_x, down_x = lax.rem(isx + 1, n_sx), lax.rem(isx + n_sx - 1, n_sx)
    ys = (lax.rem(isy + n_sy - 1, n_sy), isy, lax.rem(isy + 1, n_sy))
    other = 1 - igr
    n_low = min(4, n_sy)
    n_far = n_sy // n_low * n_grp
    low, high = lax.rem(isy, n_low), isy // n_low
    far = high * n_grp + igr

    def in_sx(k):
        return lax.rem(isx + k, n_sx)

    def in_low(k):
        return lax.rem(low + k, n_low)

    def in_far(k):
        return lax.rem(far + k, n_far)

    def at_sx(i):
        return (i, isy, igr)

    def at_low(i):
        return (isx, high * n_low + i, igr)

    def at_far(i):
        return (isx, i // n_grp * n_low + low, lax.rem(i, n_grp))

    loads = [
        pltpu.make_async_copy(vel_in, vel, ins.at[0]),
        pltpu.make_async_copy(tgt_in, tgt, ins.at[1]),
    ]
    for copy in loads:
        copy.start()

    barrier = pltpu.get_barrier_semaphore()

    def greet(device):
        pl.semaphore_signal(barrier, inc=1, device_id=device, device_id_type=MESH)

    friends = [at_sx(in_sx(k)) for k in range(1, n_sx)]
    friends += [at_low(in_low(k)) for k in range(1, n_low)]
    friends += [at_far(in_far(k)) for k in range(1, n_far)]
    friends += [(isx, ys[0], igr), (isx, ys[2], igr)]
    friends += [(to_x, to_y, igr) for to_x in (up_x, down_x) for to_y in (ys[0], ys[2])]
    for device in friends:
        greet(device)

    def remote(src, dst, send, recv, device):
        return pltpu.make_async_remote_copy(
            src_ref=src, dst_ref=dst, send_sem=send, recv_sem=recv,
            device_id=device, device_id_type=MESH,
        )

    def all_of(buffer, send, recv):
        return remote(buffer, buffer, send, recv, at_sx(in_sx(1)))

    prep[...] = jnp.zeros(prep.shape, f32)
    for c in range(3):
        for a in range(3):
            prep[a * BLK + c * 3 : a * BLK + c * 3 + 3, :] = wc[
                c * 9 + 3 * a : c * 9 + 3 * a + 3, :
            ].astype(f32)
    prep[9:10, :] = bc[...]
    w1 = prep[...][0:48, :]
    w2h = wm[...].astype(f32) * 0.5
    row48 = rows((48, 128))
    conv_high, conv_low = split(w1 * lam)
    pad = jnp.zeros((32, 128), f32)
    cw[...] = jnp.concatenate([conv_high, conv_low, pad], axis=0).T.astype(bf16)
    comp = dot(w1 * lam, w2h, HIGH)
    comp = comp + jnp.where(row48 == 9, lam * bm[...], 0.0)
    comp_high, comp_low = split(comp)
    pick = (lanes((16, 6)) == rows((16, 6))) | (lanes((16, 6)) + 8 == rows((16, 6)))
    wo_rows = dot(pick.astype(bf16), wo[...])
    ow[...] = jnp.where(rows((16, 128)) < 8, wo_rows, 0.0).astype(bf16)
    prep[...] = jnp.zeros(prep.shape, f32)
    prep[0:16, :] = wo_rows
    wo16 = prep[...].T[:, 0:16]
    outl = dot(jnp.concatenate([w2h, comp], axis=0), wo16, HIGH)
    out_high, out_low = split(outl)
    outl = jnp.where(lanes((176, 16)) < 8, out_high, out_low)
    mw[0:128, 0:128] = w2h.T.astype(bf16)
    tail = jnp.concatenate([comp_high, comp_low, pad], axis=0)
    mw[0:128, 128:256] = tail.T.astype(bf16)
    prep2[...] = jnp.zeros(prep2.shape, f32)
    prep2[0:176, 0:16] = outl
    mw[128:144, 0:128] = prep2[0:128, :].T[0:16, :].astype(bf16)
    mw[128:144, 128:256] = prep2[128:256, :].T[0:16, :].astype(bf16)
    bh, rest = split(lam * bm[...])
    bmid, rest = split(rest)
    row128 = rows((128, 128))
    t2 = jnp.where(row128 == 9, bh, jnp.where(row128 == 10, bmid, jnp.where(row128 == 11, rest, 0.0)))
    tw2[:, 0:128] = w2h.T.astype(bf16)
    tw2[:, 128:256] = t2.T.astype(bf16)
    wb2[...] = w2h.astype(bf16)
    wbo[...] = (0.5 * jnp.where(lanes((128, 16)) < 8, wo16, 0.0)).astype(bf16)

    loads[0].wait()
    for c in range(3):
        for side, x in ((0, 0), (1, CX - 1)):
            rowsrc[side, 8 * c : 8 * c + 8, :] = vel[pl.ds(c * PZ * CX + x, PZ, stride=CX), :]
        for side, p in ((0, PZ - 1), (1, 0)):
            zsrc[(side * 3 + c) * CX : (side * 3 + c + 1) * CX, :] = vel[pl.ds((c * PZ + p) * CX, CX), :]
    lane = lanes((CX, CY))

    def pack_cols(p, acc):
        for c in range(3):
            j = c * PZ + p
            v = vel[pl.ds(pl.multiple_of(j * CX, CX), CX), :]
            acc = jnp.where(lane // 2 == j, pltpu.roll(v, 2 * j + 1, 1), acc)
        return acc

    colsrc[...] = lax.fori_loop(0, PZ, pack_cols, jnp.zeros((CX, CY), f32))

    halo = []
    for d in (-1, 0, 1):
        for side, to_x in ((0, up_x), (1, down_x)):
            slot = side * 3 + 1 - d
            halo.append(
                remote(
                    rowsrc.at[1 - side], hdst.at[pl.ds(slot * 24, 24)],
                    hs.at[0], hrv.at[0], (to_x, ys[1 + d], igr),
                )
            )
    for side, to_y in ((0, ys[2]), (1, ys[0])):
        halo.append(
            remote(
                colsrc, hdst.at[pl.ds(144 + side * CX, CX)],
                hs.at[0], hrv.at[0], (isx, to_y, igr),
            )
        )
    halo_all = all_of(hdst, hs.at[0], hrv.at[0])
    halo_z = remote(zsrc, zdst, hs.at[1], hrv.at[1], (isx, isy, other))

    def enter():
        pl.semaphore_wait(barrier, len(friends))
        for copy in halo:
            copy.start()
        halo_z.start()

    loads[1].wait()
    names = tmap[...]
    place = lanes(names.shape)

    def scale_of(s):
        dest = jnp.sum(jnp.where(place == isy * S + s, names, 0), axis=1, keepdims=True)
        count = jnp.sum((names == dest).astype(f32), axis=1, keepdims=True)
        return 2.0 * gscale / count

    scales = [scale_of(s) for s in range(S)]

    sf[...] = jnp.ones(sf.shape, f32)
    zero8 = jnp.zeros((8, 128), f32)
    tg[...] = jnp.zeros(tg.shape, f32)
    for s in range(S):
        chosen = lax.broadcasted_iota(jnp.int32, (PZ, CX, CY), 0) == offs[s]

        def plane(ref, c, chosen=chosen):
            stack = ref[c * PZ * CX : (c + 1) * PZ * CX, :].reshape(PZ, CX, CY)
            return jnp.sum(jnp.where(chosen, stack, 0.0), axis=0)

        for side in (0, CX + 1):
            at = s * PLANE + side * BLK
            sf[at : at + 8, :] = zero8
            sf[at + 8 : at + 9, :] = zero8[0:1]
        for c in range(3):
            v = plane(vel, c)
            for b in range(3):
                if b == 0:
                    w = jnp.where(lane == 0, 0.0, pltpu.roll(v, 1, 1))
                elif b == 2:
                    w = jnp.where(lane == CY - 1, 0.0, pltpu.roll(v, CY - 1, 1))
                else:
                    w = v
                sf[pl.ds(s * PLANE + BLK + c * 3 + b, CX, stride=BLK), :] = w
        for c in range(6):
            tg[pl.ds(s * CX * TROW + c, CX, stride=TROW), :] = scales[s] * plane(tgt, c)
    sb[...] = sf[...].astype(bf16)
    grad[...] = jnp.zeros(grad.shape, f32)

    def sample_patches(k):
        s, part = k // PER, k % PER
        return load_patches(sb, s * PLANE + part * (XC * BLK), XC)

    def train_conv(k):
        pats = sample_patches(k)
        m = dot(cw[:, 0:96], jnp.concatenate([pats, pats], axis=0))
        h1[k], d1[k] = gate_and_slope(m)

    def train_mix(k):
        pats = sample_patches(k)
        h2[k], d2[k] = gate_and_slope(
            dot(tw2[:, 0:144], jnp.concatenate([h1[k], pats[0:16]], axis=0))
        )

    def train_out(k):
        s, part = k // PER, k % PER
        tau = dot(ow[...], h2[k])[0:8] * (scales[s] * (0.5 / lam))
        at = s * (CX * TROW) + part * (XC * TROW)
        target = jnp.concatenate(
            [tg[at + x * TROW : at + (x + 1) * TROW, :] for x in range(XC)], axis=1
        )
        err = jnp.concatenate([tau - target, jnp.zeros((8, NC), f32)], axis=0).astype(bf16)
        g2[k] = dot(wbo[...], err).astype(bf16) * d2[k]
        grad[176:184, :] += dot_nt(err, h2[k])[0:8]

    def train_back(k):
        pats = sample_patches(k)
        g1 = dot(wb2[...], g2[k]).astype(bf16) * d1[k]
        mix = dot_nt(jnp.concatenate([h1[k], pats[0:16]], axis=0), g2[k])
        grad[0:128, :] += mix[0:128]
        grad[184:192, :] += mix[136:144]
        grad[128:176, :] += dot_nt(pats, g1)

    parts = S * PER
    for k in range(parts + 3):
        if 0 <= k - 3:
            train_back(k - 3)
        if 0 <= k - 2 < parts:
            train_out(k - 2)
        if 0 <= k - 1 < parts:
            train_mix(k - 1)
        if k < parts:
            train_conv(k)
        if k == 2:
            enter()
    grad[0:128, :] = grad[0:128, :] * (0.5 / lam)
    grad[176:184, :] = grad[176:184, :] * (0.5 / lam)

    seg = GROWS // n_sx

    def seg_at(i):
        return pl.ds(pl.multiple_of(i * seg, 8), seg)

    scatter = [
        remote(grad.at[seg_at(in_sx(k))], ra.at[isx], rs.at[0], rr.at[0], at_sx(in_sx(k)))
        for k in range(1, n_sx)
    ]
    scatter_all = all_of(ra.at[pl.ds(0, n_sx - 1)], rs.at[0], rr.at[0])
    near = [
        remote(part_a, rb.at[low], rs.at[1], rr.at[1], at_low(in_low(k)))
        for k in range(1, n_low)
    ]
    near_all = all_of(rb.at[pl.ds(0, n_low - 1)], rs.at[1], rr.at[1])
    wide = [
        remote(part_b, rc.at[far], rs.at[2], rr.at[2], at_far(in_far(k)))
        for k in range(1, n_far)
    ]
    wide_all = all_of(rc.at[pl.ds(0, n_far - 1)], rs.at[2], rr.at[2])
    gather = [
        remote(part_c, rd.at[isx], rs.at[3], rr.at[3], at_sx(in_sx(k)))
        for k in range(1, n_sx)
    ]
    gather_all = all_of(rd.at[pl.ds(0, n_sx - 1)], rs.at[3], rr.at[3])

    def total_of(buffer, count):
        total = buffer[0]
        for j in range(1, count):
            total = total + buffer[j]
        return total

    ra[isx] = grad[seg_at(isx), :]
    for copy in scatter:
        copy.start()

    def second():
        scatter_all.wait_recv()
        total = total_of(ra, n_sx)
        part_a[...] = total
        rb[low] = total
        for copy in near:
            copy.start()

    def third():
        near_all.wait_recv()
        total = total_of(rb, n_low)
        part_b[...] = total
        rc[far] = total
        for copy in wide:
            copy.start()

    def fourth():
        wide_all.wait_recv()
        total = total_of(rc, n_far)
        part_c[...] = total
        rd[isx] = total
        for copy in gather:
            copy.start()

    qf[...] = jnp.ones(qf.shape, f32)
    halo_all.wait_recv()
    lane24 = lanes((24, CY))
    for side in (0, 1):
        left, mid, right = (hdst[(side * 3 + i) * 24 : (side * 3 + i + 1) * 24, :] for i in range(3))
        shifted = (
            jnp.where(lane24 == 0, pltpu.roll(left, 1, 1), pltpu.roll(mid, 1, 1)),
            mid,
            jnp.where(
                lane24 == CY - 1, pltpu.roll(right, CY - 1, 1), pltpu.roll(mid, CY - 1, 1)
            ),
        )
        at = side * (CX + 1) * BLK
        for b in range(3):
            hr[...] = shifted[b]
            for c in range(3):
                qf[pl.ds(at + c * 3 + b, PZ, stride=PLANE), :] = hr[8 * c : 8 * c + 8, :]
    cc[...] = jnp.where(
        lax.rem(lane, 2) == 0, pltpu.roll(hdst[176:208, :], CY - 1, 1), pltpu.roll(hdst[144:176, :], 1, 1)
    )

    def build(p):
        for c in range(3):
            j = c * PZ + p
            v = vel[pl.ds(pl.multiple_of(j * CX, CX), CX), :]
            edge = pltpu.roll(cc[...], CY - 1 - 2 * j, 1)
            at = p * PLANE + BLK + c * 3
            qf[pl.ds(at, CX, stride=BLK), :] = jnp.where(lane == 0, edge, pltpu.roll(v, 1, 1))
            qf[pl.ds(at + 1, CX, stride=BLK), :] = v
            qf[pl.ds(at + 2, CX, stride=BLK), :] = jnp.where(
                lane == CY - 1, edge, pltpu.roll(v, CY - 1, 1)
            )
        base = pl.ds(pl.multiple_of(p * PLANE, BLK), PLANE)
        qb[base, :] = qf[base, :].astype(bf16)

    def patches_of(k):
        return load_patches(qb, ORDER[k // PER] * PLANE + (k % PER) * (XC * BLK), XC)

    def stage_conv(k):
        pats = patches_of(k)
        q1[k % 2] = gate(dot(cw[:, 0:96], jnp.concatenate([pats, pats], axis=0)))

    def stage_mix(k):
        pats = patches_of(k)
        m2 = dot(mw[:, 0:224], jnp.concatenate([q1[k % 2], pats, pats], axis=0))
        q2[k % 2] = gate(m2[0:128])
        lin[k % 2] = m2[128:136] + m2[136:144]

    def stage_out(k):
        tau = dot(ow[...], q2[k % 2])[0:8] + lin[k % 2]
        at = (ORDER[k // PER] + 1) * TPLANE + (k % PER * XC + 1) * TROW
        for x in range(XC):
            stress[at + x * TROW : at + (x + 1) * TROW, :] = tau[:, x * CY : (x + 1) * CY]

    zs = [
        remote(
            stress.at[pl.ds(p * TPLANE + TROW, CX * TROW)],
            stress.at[pl.ds((PZ + 1) * side * TPLANE + TROW, CX * TROW)],
            ss.at[2], srv.at[2], (isx, isy, other),
        )
        for side, p in ((0, PZ), (1, 1))
    ]
    zs_all = all_of(stress.at[pl.ds(0, 2 * CX * TROW)], ss.at[2], srv.at[2])

    scolsrc[...] = jnp.zeros(scolsrc.shape, f32)
    srowsrc[...] = jnp.zeros(srowsrc.shape, f32)

    def edge_copies(group):
        out = [
            remote(
                srowsrc.at[group, 1 - side], edst.at[group, pl.ds(side * 24, 24)],
                ss.at[group], srv.at[group], (to_x, isy, igr),
            )
            for side, to_x in ((0, up_x), (1, down_x))
        ]
        return out + [
            remote(
                scolsrc.at[group], edst.at[group, pl.ds(48 + side * CX, CX)],
                ss.at[group], srv.at[group], (isx, to_y, igr),
            )
            for side, to_y in ((0, ys[2]), (1, ys[0]))
        ]

    edges = [edge_copies(0), edge_copies(1)]
    edges_all = [all_of(edst.at[g], ss.at[g], srv.at[g]) for g in (0, 1)]
    groups = (ORDER[:EARLY], ORDER[EARLY:])

    def send_edges(group):
        acc = jnp.zeros((CX, CY), f32)
        for p in groups[group]:
            for c in range(3):
                j = c * PZ + p
                at = (p + 1) * TPLANE
                for side, x in ((0, 1), (1, CX)):
                    srowsrc[group, side, j : j + 1, :] = stress[
                        at + x * TROW + DX[c] : at + x * TROW + DX[c] + 1, :
                    ]
                v = stress[pl.ds(at + TROW + DY[c], CX, stride=TROW), :]
                acc = jnp.where(lane // 2 == j, pltpu.roll(v, 2 * j + 1, 1), acc)
        scolsrc[group] = acc
        for copy in edges[group]:
            copy.start()

    chunks = PZ * PER
    build(ORDER[0])
    for k in range(chunks + 2):
        if k % PER == 0 and k // PER + 1 < PZ:
            build(ORDER[k // PER + 1])
        if 0 <= k - 2:
            stage_out(k - 2)
        if 0 <= k - 1 < chunks:
            stage_mix(k - 1)
        if k < chunks:
            stage_conv(k)
        if k - 2 == 2 * PER - 1:
            for copy in zs:
                copy.start()
        if k - 2 == EARLY * PER - 1:
            send_edges(0)
        if k == 6:
            second()
        if k == 9:
            third()
        if k == 13:
            fourth()
    send_edges(1)

    halo_z.wait_recv()

    def viscous(p, below, above):
        for c in range(3):
            at = p * PLANE + BLK + c * 3

            def pick_at(start):
                return qf[pl.ds(start, CX, stride=BLK), :]

            mid = pick_at(at + 1)
            total = pick_at(at) + pick_at(at + 2)
            total = total + pick_at(at + 1 - BLK) + pick_at(at + 1 + BLK)
            total = total + below(c) + above(c) - 6.0 * mid
            tend[pl.ds(pl.multiple_of((c * PZ + p) * CX, CX), CX), :] = visc * total

    def plane_of(p):
        return lambda c: vel[pl.ds(pl.multiple_of((c * PZ + p) * CX, CX), CX), :]

    def ghost(side):
        return lambda c: zdst[(side * 3 + c) * CX : (side * 3 + c + 1) * CX, :]

    viscous(0, ghost(0), plane_of(1))

    def inner(p, _):
        viscous(p, plane_of(p - 1), plane_of(p + 1))
        return 0

    lax.fori_loop(1, PZ - 1, inner, 0)
    viscous(PZ - 1, plane_of(PZ - 2), ghost(1))

    gather_all.wait_recv()
    scatter_all.wait_send()
    for j in range(n_sx):
        grad[j * seg : (j + 1) * seg, :] = rd[j]
    gmix[...] = grad[0:128, :]
    for c in range(3):
        for a in range(3):
            at = 128 + a * BLK + c * 3
            gconv[c * 9 + 3 * a : c * 9 + 3 * a + 3, :] = grad[at : at + 3, :]
    gbconv[...] = grad[137:138, :]
    gbmix[...] = grad[185:186, :]
    gout[...] = grad[176:182, :]

    half = 0.25 / lam

    def diverge(p):
        for c in range(3):
            j = c * PZ + p

            def pick_at(plane, x, comp):
                return stress[pl.ds((p + plane) * TPLANE + x * TROW + comp, CX, stride=TROW), :]

            along_x = pick_at(1, 2, DX[c]) - pick_at(1, 0, DX[c])
            v = pick_at(1, 1, DY[c])
            edge = pltpu.roll(scc[...], CY - 1 - 2 * j, 1)
            along_y = jnp.where(lane == CY - 1, edge, pltpu.roll(v, CY - 1, 1)) - jnp.where(
                lane == 0, edge, pltpu.roll(v, 1, 1)
            )
            along_z = pick_at(2, 1, DZ[c]) - pick_at(0, 1, DZ[c])
            at = pl.ds(j * CX, CX)
            tend[at, :] = tend[at, :] - half * (along_x + along_y + along_z)

    zs_all.wait_send()
    zs_all.wait_recv()
    for group in (0, 1):
        edges_all[group].wait_recv()
        for p in groups[group]:
            for side in (0, 1):
                for c in range(3):
                    at = (p + 1) * TPLANE + side * (CX + 1) * TROW + DX[c]
                    stress[at : at + 1, :] = edst[
                        group, side * 24 + c * PZ + p : side * 24 + c * PZ + p + 1, :
                    ]
        scc[...] = jnp.where(
            lax.rem(lane, 2) == 0,
            pltpu.roll(edst[group, 80:112, :], CY - 1, 1),
            pltpu.roll(edst[group, 48:80, :], 1, 1),
        )
        for p in groups[group]:
            diverge(p)

    for group in (halo_all, halo_z, *edges_all, near_all, wide_all, gather_all):
        group.wait_send()


def write_out(*refs):
    for source, result in zip(refs[:6], refs[6:]):
        result[...] = source[...]


def shards(velocity, target_stress, w_conv, b_conv, w_mix, b_mix, w_out, plane_offsets, trainer_map):
    n_sx, n_sy, n_grp = (lax.axis_size(a) for a in ("sx", "sy", "grp"))
    n_low = min(4, n_sy)
    n_far = n_sy // n_low * n_grp
    seg = GROWS // n_sx
    gscale = 1.0 / math.sqrt(S * n_sx * n_sy * n_grp * CX * CY)
    vmem = pl.BlockSpec(memory_space=pltpu.VMEM)
    smem = pl.BlockSpec(memory_space=pltpu.SMEM)
    hbm = pl.BlockSpec(memory_space=pltpu.HBM)

    def buf(*shape, dtype=f32):
        return pltpu.VMEM(shape, dtype)

    def sems(count):
        return pltpu.SemaphoreType.DMA((count,))

    outs = pl.pallas_call(
        functools.partial(kernel, n_sx, n_sy, n_grp, gscale),
        out_shape=[
            jax.ShapeDtypeStruct((3 * PZ * CX, CY), f32),
            jax.ShapeDtypeStruct((27, 128), f32),
            jax.ShapeDtypeStruct((1, 128), f32),
            jax.ShapeDtypeStruct((128, 128), f32),
            jax.ShapeDtypeStruct((1, 128), f32),
            jax.ShapeDtypeStruct((6, 128), f32),
        ],
        in_specs=[hbm] * 2 + [vmem] * 5 + [smem, vmem],
        out_specs=[vmem] * 6,
        scratch_shapes=[
            buf(3 * PZ * CX, CY), buf(6 * PZ * CX, CY),
            buf(PZ * PLANE, CY), buf(PZ * PLANE, CY, dtype=bf16),
            buf(S * PLANE, CY), buf(S * PLANE, CY, dtype=bf16),
            buf(S * CX * TROW, CY),
            buf((PZ + 2) * TPLANE, CY),
            buf(128, 128, dtype=bf16), buf(144, 256, dtype=bf16), buf(16, 128, dtype=bf16),
            buf(128, 256, dtype=bf16),
            buf(128, 128, dtype=bf16), buf(128, 16, dtype=bf16),
            buf(128, 128), buf(256, 128),
            buf(2, 128, NC, dtype=bf16), buf(2, 128, NC, dtype=bf16), buf(2, 8, NC),
            buf(GROWS, 128),
            *[buf(S * PER, 128, NC, dtype=bf16) for _ in range(5)],
            buf(2, 24, CY), buf(CX, CY), buf(208, CY),
            buf(6 * CX, CY), buf(6 * CX, CY),
            buf(24, CY), buf(CX, CY),
            buf(2, 2, 24, CY), buf(2, CX, CY), buf(2, 112, CY), buf(CX, CY),
            buf(n_sx, seg, 128), buf(seg, 128),
            buf(n_low, seg, 128), buf(seg, 128),
            buf(n_far, seg, 128), buf(seg, 128),
            buf(n_sx, seg, 128),
            sems(2), sems(2), sems(2), sems(3), sems(3), sems(4), sems(4),
        ],
        compiler_params=pltpu.CompilerParams(
            collective_id=0, has_side_effects=True, vmem_limit_bytes=62 * 2**20
        ),
    )(
        velocity.reshape(3 * PZ * CX, CY),
        target_stress.reshape(6 * PZ * CX, CY),
        w_conv,
        b_conv.reshape(1, 128),
        w_mix,
        b_mix.reshape(1, 128),
        w_out.T,
        plane_offsets.reshape(S),
        trainer_map.reshape(1, n_sy * S),
    )
    outs = pl.pallas_call(
        write_out,
        out_shape=[jax.ShapeDtypeStruct(o.shape, o.dtype) for o in outs],
        in_specs=[vmem] * 6,
        out_specs=[vmem] * 6,
    )(*outs)
    return (
        outs[0].reshape(3, PZ, CX, CY),
        outs[1],
        outs[2].reshape(128),
        outs[3],
        outs[4].reshape(128),
        outs[5].T,
    )


def solution(mesh):
    in_specs = (
        P(None, "grp", "sx", "sy"),
        P(None, "grp", "sx", "sy"),
        P(),
        P(),
        P(),
        P(),
        P(),
        P("grp", "sx", "sy", None),
        P("grp", "sx", None, None),
    )
    out_specs = (P(None, "grp", "sx", "sy"), P(), P(), P(), P(), P())
    return jax.shard_map(shards, mesh=mesh, in_specs=in_specs, out_specs=out_specs, check_vma=False)
```

```python
import functools
import math

import jax
import jax.numpy as jnp
from jax import lax
from jax.experimental import pallas as pl
from jax.experimental.pallas import tpu as pltpu
from jax.sharding import PartitionSpec as P

f32 = jnp.float32
bf16 = jnp.bfloat16
MESH = pl.DeviceIdType.MESH
HIGH = lax.Precision.HIGHEST

S = 2
gelu_c = 0.7978845608
gelu_k = 0.044715
visc = 0.1
lam = (gelu_c * gelu_k) ** (1.0 / 3.0)
shift_c = gelu_c / lam

PZ = 8
CX = 32
CY = 128
BLK = 16
PLANE = (CX + 2) * BLK
TROW = 8
TPLANE = (CX + 2) * TROW
XC = 16
NC = XC * CY
PER = CX // XC
ORDER = (0, 7, 1, 2, 3, 4, 5, 6)
EARLY = 6
GROWS = 192

DX = (0, 3, 4)
DY = (3, 1, 5)
DZ = (4, 5, 2)


def dot(a, b, precision=None):
    return jnp.dot(a, b, preferred_element_type=f32, precision=precision)


def dot_nt(a, b, precision=None):
    return lax.dot_general(
        a, b, (((1,), (1,)), ((), ())), preferred_element_type=f32, precision=precision
    )


def split(value):
    high = value.astype(bf16).astype(f32)
    return high, value - high


def gate(m):
    return (m * jnp.tanh(m * (m * m + shift_c))).astype(bf16)


def gate_and_slope(m):
    m = m.astype(bf16)
    z = m * (m * m + bf16(shift_c))
    t = jnp.tanh(z)
    up = bf16(1.0) + t
    down = bf16(1.0) - t
    return m * up, up * (bf16(1.0) + down * (bf16(3.0) * z - bf16(2.0 * shift_c) * m))


def lanes(shape):
    return lax.broadcasted_iota(jnp.int32, shape, 1)


def rows(shape):
    return lax.broadcasted_iota(jnp.int32, shape, 0)


def load_patches(buffer, base, count):
    return jnp.concatenate(
        [
            buffer[pl.ds(pl.multiple_of(base + x * BLK, BLK), 3 * BLK), :]
            for x in range(count)
        ],
        axis=1,
    )


def kernel(
    n_sx, n_sy, n_grp, gscale,
    vel_in, tgt_in, wc, bc, wm, bm, wo, offs, tmap,
    tend, gconv, gbconv, gmix, gbmix, gout,
    vel, tgt,
    qf, qb, sf, sb, tg, stress, cw, mw, ow, tw2, wb2, wbo, prep, prep2,
    q1, q2, lin, grad, h1, d1, h2, d2, g2,
    rowsrc, colsrc, hdst, zsrc, zdst, hr, cc,
    srowsrc, scolsrc, edst, scc, szsrc, szdst,
    gseg, ra, part_a, rb, part_b, rc,
    ins, hs, hrv, ss, srv, rs, rr,
):
    isx, isy, igr = lax.axis_index("sx"), lax.axis_index("sy"), lax.axis_index("grp")
    up_x, down_x = lax.rem(isx + 1, n_sx), lax.rem(isx + n_sx - 1, n_sx)
    ys = (lax.rem(isy + n_sy - 1, n_sy), isy, lax.rem(isy + 1, n_sy))
    other = 1 - igr
    n_b = n_sx * n_grp
    ib = isx * n_grp + igr

    def in_sy(k):
        return lax.rem(isy + k, n_sy)

    def in_b(k):
        return lax.rem(ib + k, n_b)

    def at_sy(i):
        return (isx, i, igr)

    def at_b(i):
        return (i // n_grp, isy, lax.rem(i, n_grp))

    loads = [
        pltpu.make_async_copy(vel_in, vel, ins.at[0]),
        pltpu.make_async_copy(tgt_in, tgt, ins.at[1]),
    ]
    for copy in loads:
        copy.start()

    barrier = pltpu.get_barrier_semaphore()

    def greet(device):
        pl.semaphore_signal(barrier, inc=1, device_id=device, device_id_type=MESH)

    friends = [at_sy(in_sy(k)) for k in range(1, n_sy)]
    friends += [at_b(in_b(k)) for k in range(1, n_b)]
    friends += [(to_x, to_y, igr) for to_x in (up_x, down_x) for to_y in (ys[0], ys[2])]
    for device in friends:
        greet(device)

    def remote(src, dst, send, recv, device):
        return pltpu.make_async_remote_copy(
            src_ref=src, dst_ref=dst, send_sem=send, recv_sem=recv,
            device_id=device, device_id_type=MESH,
        )

    def all_of(buffer, send, recv):
        return remote(buffer, buffer, send, recv, at_sy(in_sy(1)))

    prep[...] = jnp.zeros(prep.shape, f32)
    for c in range(3):
        for a in range(3):
            prep[a * BLK + c * 3 : a * BLK + c * 3 + 3, :] = wc[
                c * 9 + 3 * a : c * 9 + 3 * a + 3, :
            ].astype(f32)
    prep[9:10, :] = bc[...]
    w1 = prep[...][0:48, :]
    w2h = wm[...].astype(f32) * 0.5
    row48 = rows((48, 128))
    conv_high, conv_low = split(w1 * lam)
    pad = jnp.zeros((32, 128), f32)
    cw[...] = jnp.concatenate([conv_high, conv_low, pad], axis=0).T.astype(bf16)
    comp = dot(w1 * lam, w2h, HIGH)
    comp = comp + jnp.where(row48 == 9, lam * bm[...], 0.0)
    comp_high, comp_low = split(comp)
    pick = (lanes((16, 6)) == rows((16, 6))) | (lanes((16, 6)) + 8 == rows((16, 6)))
    wo_rows = dot(pick.astype(bf16), wo[...])
    ow[...] = jnp.where(rows((16, 128)) < 8, wo_rows, 0.0).astype(bf16)
    prep[...] = jnp.zeros(prep.shape, f32)
    prep[0:16, :] = wo_rows
    wo16 = prep[...].T[:, 0:16]
    outl = dot(jnp.concatenate([w2h, comp], axis=0), wo16, HIGH)
    out_high, out_low = split(outl)
    outl = jnp.where(lanes((176, 16)) < 8, out_high, out_low)
    mw[0:128, 0:128] = w2h.T.astype(bf16)
    tail = jnp.concatenate([comp_high, comp_low, pad], axis=0)
    mw[0:128, 128:256] = tail.T.astype(bf16)
    prep2[...] = jnp.zeros(prep2.shape, f32)
    prep2[0:176, 0:16] = outl
    mw[128:144, 0:128] = prep2[0:128, :].T[0:16, :].astype(bf16)
    mw[128:144, 128:256] = prep2[128:256, :].T[0:16, :].astype(bf16)
    bh, rest = split(lam * bm[...])
    bmid, rest = split(rest)
    row128 = rows((128, 128))
    t2 = jnp.where(row128 == 9, bh, jnp.where(row128 == 10, bmid, jnp.where(row128 == 11, rest, 0.0)))
    tw2[:, 0:128] = w2h.T.astype(bf16)
    tw2[:, 128:256] = t2.T.astype(bf16)
    wb2[...] = w2h.astype(bf16)
    wbo[...] = (0.5 * jnp.where(lanes((128, 16)) < 8, wo16, 0.0)).astype(bf16)

    loads[0].wait()
    for c in range(3):
        for side, x in ((0, 0), (1, CX - 1)):
            rowsrc[side, 8 * c : 8 * c + 8, :] = vel[pl.ds(c * PZ * CX + x, PZ, stride=CX), :]
        for side, p in ((0, PZ - 1), (1, 0)):
            zsrc[(side * 3 + c) * CX : (side * 3 + c + 1) * CX, :] = vel[pl.ds((c * PZ + p) * CX, CX), :]
    lane = lanes((CX, CY))

    def pack_cols(p, acc):
        for c in range(3):
            j = c * PZ + p
            v = vel[pl.ds(pl.multiple_of(j * CX, CX), CX), :]
            acc = jnp.where(lane // 2 == j, pltpu.roll(v, 2 * j + 1, 1), acc)
        return acc

    colsrc[...] = lax.fori_loop(0, PZ, pack_cols, jnp.zeros((CX, CY), f32))

    halo = []
    for d in (-1, 0, 1):
        for side, to_x in ((0, up_x), (1, down_x)):
            slot = side * 3 + 1 - d
            halo.append(
                remote(
                    rowsrc.at[1 - side], hdst.at[pl.ds(slot * 24, 24)],
                    hs.at[0], hrv.at[0], (to_x, ys[1 + d], igr),
                )
            )
    for side, to_y in ((0, ys[2]), (1, ys[0])):
        halo.append(
            remote(
                colsrc, hdst.at[pl.ds(144 + side * CX, CX)],
                hs.at[0], hrv.at[0], (isx, to_y, igr),
            )
        )
    halo_all = all_of(hdst, hs.at[0], hrv.at[0])
    halo_z = remote(zsrc, zdst, hs.at[1], hrv.at[1], (isx, isy, other))

    def enter():
        pl.semaphore_wait(barrier, len(friends))
        for copy in halo:
            copy.start()
        halo_z.start()

    loads[1].wait()
    names = tmap[...]
    place = lanes(names.shape)

    def scale_of(s):
        dest = jnp.sum(jnp.where(place == isy * S + s, names, 0), axis=1, keepdims=True)
        count = jnp.sum((names == dest).astype(f32), axis=1, keepdims=True)
        return 2.0 * gscale / count

    scales = [scale_of(s) for s in range(S)]

    sf[...] = jnp.ones(sf.shape, f32)
    zero8 = jnp.zeros((8, 128), f32)
    tg[...] = jnp.zeros(tg.shape, f32)
    for s in range(S):
        chosen = lax.broadcasted_iota(jnp.int32, (PZ, CX, CY), 0) == offs[s]

        def plane(ref, c, chosen=chosen):
            stack = ref[c * PZ * CX : (c + 1) * PZ * CX, :].reshape(PZ, CX, CY)
            return jnp.sum(jnp.where(chosen, stack, 0.0), axis=0)

        for side in (0, CX + 1):
            at = s * PLANE + side * BLK
            sf[at : at + 8, :] = zero8
            sf[at + 8 : at + 9, :] = zero8[0:1]
        for c in range(3):
            v = plane(vel, c)
            for b in range(3):
                if b == 0:
                    w = jnp.where(lane == 0, 0.0, pltpu.roll(v, 1, 1))
                elif b == 2:
                    w = jnp.where(lane == CY - 1, 0.0, pltpu.roll(v, CY - 1, 1))
                else:
                    w = v
                sf[pl.ds(s * PLANE + BLK + c * 3 + b, CX, stride=BLK), :] = w
        for c in range(6):
            tg[pl.ds(s * CX * TROW + c, CX, stride=TROW), :] = scales[s] * plane(tgt, c)
    sb[...] = sf[...].astype(bf16)
    grad[...] = jnp.zeros(grad.shape, f32)

    def sample_patches(k):
        s, part = k // PER, k % PER
        return load_patches(sb, s * PLANE + part * (XC * BLK), XC)

    def train_conv(k):
        pats = sample_patches(k)
        m = dot(cw[:, 0:96], jnp.concatenate([pats, pats], axis=0))
        h1[k], d1[k] = gate_and_slope(m)

    def train_mix(k):
        pats = sample_patches(k)
        h2[k], d2[k] = gate_and_slope(
            dot(tw2[:, 0:144], jnp.concatenate([h1[k], pats[0:16]], axis=0))
        )

    def train_out(k):
        s, part = k // PER, k % PER
        tau = dot(ow[...], h2[k])[0:8] * (scales[s] * (0.5 / lam))
        at = s * (CX * TROW) + part * (XC * TROW)
        target = jnp.concatenate(
            [tg[at + x * TROW : at + (x + 1) * TROW, :] for x in range(XC)], axis=1
        )
        err = jnp.concatenate([tau - target, jnp.zeros((8, NC), f32)], axis=0).astype(bf16)
        g2[k] = dot(wbo[...], err).astype(bf16) * d2[k]
        grad[176:184, :] += dot_nt(err, h2[k])[0:8]

    def train_back(k):
        pats = sample_patches(k)
        g1 = dot(wb2[...], g2[k]).astype(bf16) * d1[k]
        mix = dot_nt(jnp.concatenate([h1[k], pats[0:16]], axis=0), g2[k])
        grad[0:128, :] += mix[0:128]
        grad[184:192, :] += mix[136:144]
        grad[128:176, :] += dot_nt(pats, g1)

    parts = S * PER
    for k in range(parts + 3):
        if 0 <= k - 3:
            train_back(k - 3)
        if 0 <= k - 2 < parts:
            train_out(k - 2)
        if 0 <= k - 1 < parts:
            train_mix(k - 1)
        if k < parts:
            train_conv(k)
        if k == 2:
            enter()
    grad[0:128, :] = grad[0:128, :] * (0.5 / lam)
    grad[176:184, :] = grad[176:184, :] * (0.5 / lam)

    seg = GROWS // n_sy
    for j in range(n_sy):
        gseg[j] = grad[j * seg : (j + 1) * seg, :]
    scatter = [
        remote(gseg.at[in_sy(k)], ra.at[isy], rs.at[0], rr.at[0], at_sy(in_sy(k)))
        for k in range(1, n_sy)
    ]
    scatter_all = all_of(ra.at[pl.ds(0, n_sy - 1)], rs.at[0], rr.at[0])
    wide = [
        remote(part_a, rb.at[ib], rs.at[1], rr.at[1], at_b(in_b(k))) for k in range(1, n_b)
    ]
    wide_all = all_of(rb.at[pl.ds(0, n_b - 1)], rs.at[1], rr.at[1])
    gather = [
        remote(part_b, rc.at[isy], rs.at[2], rr.at[2], at_sy(in_sy(k))) for k in range(1, n_sy)
    ]
    gather_all = all_of(rc.at[pl.ds(0, n_sy - 1)], rs.at[2], rr.at[2])

    def total_of(buffer, count):
        total = buffer[0]
        for j in range(1, count):
            total = total + buffer[j]
        return total

    ra[isy] = gseg[isy]
    for copy in scatter:
        copy.start()

    def second():
        scatter_all.wait_recv()
        total = total_of(ra, n_sy)
        part_a[...] = total
        rb[ib] = total
        for copy in wide:
            copy.start()

    def third():
        wide_all.wait_recv()
        total = total_of(rb, n_b)
        part_b[...] = total
        rc[isy] = total
        for copy in gather:
            copy.start()

    qf[...] = jnp.ones(qf.shape, f32)
    halo_all.wait_recv()
    lane24 = lanes((24, CY))
    for side in (0, 1):
        left, mid, right = (hdst[(side * 3 + i) * 24 : (side * 3 + i + 1) * 24, :] for i in range(3))
        shifted = (
            jnp.where(lane24 == 0, pltpu.roll(left, 1, 1), pltpu.roll(mid, 1, 1)),
            mid,
            jnp.where(
                lane24 == CY - 1, pltpu.roll(right, CY - 1, 1), pltpu.roll(mid, CY - 1, 1)
            ),
        )
        at = side * (CX + 1) * BLK
        for b in range(3):
            hr[...] = shifted[b]
            for c in range(3):
                qf[pl.ds(at + c * 3 + b, PZ, stride=PLANE), :] = hr[8 * c : 8 * c + 8, :]
    cc[...] = jnp.where(
        lax.rem(lane, 2) == 0, pltpu.roll(hdst[176:208, :], CY - 1, 1), pltpu.roll(hdst[144:176, :], 1, 1)
    )

    def build(p):
        for c in range(3):
            j = c * PZ + p
            v = vel[pl.ds(pl.multiple_of(j * CX, CX), CX), :]
            edge = pltpu.roll(cc[...], CY - 1 - 2 * j, 1)
            at = p * PLANE + BLK + c * 3
            qf[pl.ds(at, CX, stride=BLK), :] = jnp.where(lane == 0, edge, pltpu.roll(v, 1, 1))
            qf[pl.ds(at + 1, CX, stride=BLK), :] = v
            qf[pl.ds(at + 2, CX, stride=BLK), :] = jnp.where(
                lane == CY - 1, edge, pltpu.roll(v, CY - 1, 1)
            )
        base = pl.ds(pl.multiple_of(p * PLANE, BLK), PLANE)
        qb[base, :] = qf[base, :].astype(bf16)

    def patches_of(k):
        return load_patches(qb, ORDER[k // PER] * PLANE + (k % PER) * (XC * BLK), XC)

    def stage_conv(k):
        pats = patches_of(k)
        q1[k % 2] = gate(dot(cw[:, 0:96], jnp.concatenate([pats, pats], axis=0)))

    def stage_mix(k):
        pats = patches_of(k)
        m2 = dot(mw[:, 0:224], jnp.concatenate([q1[k % 2], pats, pats], axis=0))
        q2[k % 2] = gate(m2[0:128])
        lin[k % 2] = m2[128:136] + m2[136:144]

    def stage_out(k):
        tau = dot(ow[...], q2[k % 2])[0:8] + lin[k % 2]
        at = ORDER[k // PER] * TPLANE + (k % PER * XC + 1) * TROW
        for x in range(XC):
            stress[at + x * TROW : at + (x + 1) * TROW, :] = tau[:, x * CY : (x + 1) * CY]

    zs = remote(szsrc, szdst, ss.at[2], srv.at[2], (isx, isy, other))

    def send_z():
        for side, p in ((0, PZ - 1), (1, 0)):
            for c in range(3):
                at = (side * 3 + c) * CX
                szsrc[at : at + CX, :] = stress[
                    pl.ds(p * TPLANE + TROW + DZ[c], CX, stride=TROW), :
                ]
        zs.start()

    scolsrc[...] = jnp.zeros(scolsrc.shape, f32)
    srowsrc[...] = jnp.zeros(srowsrc.shape, f32)

    def edge_copies(group):
        out = [
            remote(
                srowsrc.at[group, 1 - side], edst.at[group, pl.ds(side * 24, 24)],
                ss.at[group], srv.at[group], (to_x, isy, igr),
            )
            for side, to_x in ((0, up_x), (1, down_x))
        ]
        return out + [
            remote(
                scolsrc.at[group], edst.at[group, pl.ds(48 + side * CX, CX)],
                ss.at[group], srv.at[group], (isx, to_y, igr),
            )
            for side, to_y in ((0, ys[2]), (1, ys[0]))
        ]

    edges = [edge_copies(0), edge_copies(1)]
    edges_all = [all_of(edst.at[g], ss.at[g], srv.at[g]) for g in (0, 1)]
    groups = (ORDER[:EARLY], ORDER[EARLY:])

    def send_edges(group):
        acc = jnp.zeros((CX, CY), f32)
        for p in groups[group]:
            for c in range(3):
                j = c * PZ + p
                at = p * TPLANE
                for side, x in ((0, 1), (1, CX)):
                    srowsrc[group, side, j : j + 1, :] = stress[
                        at + x * TROW + DX[c] : at + x * TROW + DX[c] + 1, :
                    ]
                v = stress[pl.ds(at + TROW + DY[c], CX, stride=TROW), :]
                acc = jnp.where(lane // 2 == j, pltpu.roll(v, 2 * j + 1, 1), acc)
        scolsrc[group] = acc
        for copy in edges[group]:
            copy.start()

    chunks = PZ * PER
    build(ORDER[0])
    for k in range(chunks + 2):
        if k % PER == 0 and k // PER + 1 < PZ:
            build(ORDER[k // PER + 1])
        if 0 <= k - 2:
            stage_out(k - 2)
        if 0 <= k - 1 < chunks:
            stage_mix(k - 1)
        if k < chunks:
            stage_conv(k)
        if k == 14:
            send_z()
        if k - 2 == EARLY * PER - 1:
            send_edges(0)
        if k == 6:
            second()
        if k == 13:
            third()
    send_edges(1)

    halo_z.wait_recv()

    def viscous(p, below, above):
        for c in range(3):
            at = p * PLANE + BLK + c * 3

            def pick_at(start):
                return qf[pl.ds(start, CX, stride=BLK), :]

            mid = pick_at(at + 1)
            total = pick_at(at) + pick_at(at + 2)
            total = total + pick_at(at + 1 - BLK) + pick_at(at + 1 + BLK)
            total = total + below(c) + above(c) - 6.0 * mid
            tend[pl.ds(pl.multiple_of((c * PZ + p) * CX, CX), CX), :] = visc * total

    def plane_of(p):
        return lambda c: vel[pl.ds(pl.multiple_of((c * PZ + p) * CX, CX), CX), :]

    def ghost(side):
        return lambda c: zdst[(side * 3 + c) * CX : (side * 3 + c + 1) * CX, :]

    viscous(0, ghost(0), plane_of(1))

    def inner(p, _):
        viscous(p, plane_of(p - 1), plane_of(p + 1))
        return 0

    lax.fori_loop(1, PZ - 1, inner, 0)
    viscous(PZ - 1, plane_of(PZ - 2), ghost(1))

    half = 0.25 / lam

    def diverge(p):
        for c in range(3):
            j = c * PZ + p

            def pick_at(plane, x, comp):
                if plane < 0 or plane == PZ:
                    side = 0 if plane < 0 else 1
                    return szdst[(side * 3 + c) * CX : (side * 3 + c + 1) * CX, :]
                return stress[pl.ds(plane * TPLANE + x * TROW + comp, CX, stride=TROW), :]

            along_x = pick_at(p, 2, DX[c]) - pick_at(p, 0, DX[c])
            v = pick_at(p, 1, DY[c])
            edge = pltpu.roll(scc[...], CY - 1 - 2 * j, 1)
            along_y = jnp.where(lane == CY - 1, edge, pltpu.roll(v, CY - 1, 1)) - jnp.where(
                lane == 0, edge, pltpu.roll(v, 1, 1)
            )
            along_z = pick_at(p + 1, 1, DZ[c]) - pick_at(p - 1, 1, DZ[c])
            at = pl.ds(j * CX, CX)
            tend[at, :] = tend[at, :] - half * (along_x + along_y + along_z)

    zs.wait_recv()
    for group in (0, 1):
        edges_all[group].wait_recv()
        for p in groups[group]:
            for side in (0, 1):
                for c in range(3):
                    at = p * TPLANE + side * (CX + 1) * TROW + DX[c]
                    stress[at : at + 1, :] = edst[
                        group, side * 24 + c * PZ + p : side * 24 + c * PZ + p + 1, :
                    ]
        scc[...] = jnp.where(
            lax.rem(lane, 2) == 0,
            pltpu.roll(edst[group, 80:112, :], CY - 1, 1),
            pltpu.roll(edst[group, 48:80, :], 1, 1),
        )
        for p in groups[group]:
            diverge(p)

    gather_all.wait_recv()
    for j in range(n_sy):
        grad[j * seg : (j + 1) * seg, :] = rc[j]
    gmix[...] = grad[0:128, :]
    for c in range(3):
        for a in range(3):
            at = 128 + a * BLK + c * 3
            gconv[c * 9 + 3 * a : c * 9 + 3 * a + 3, :] = grad[at : at + 3, :]
    gbconv[...] = grad[137:138, :]
    gbmix[...] = grad[185:186, :]
    gout[...] = grad[176:182, :]

    for group in (halo_all, halo_z, zs, *edges_all, scatter_all, wide_all, gather_all):
        group.wait_send()


def write_out(*refs):
    for source, result in zip(refs[:6], refs[6:]):
        result[...] = source[...]


def shards(velocity, target_stress, w_conv, b_conv, w_mix, b_mix, w_out, plane_offsets, trainer_map):
    n_sx, n_sy, n_grp = (lax.axis_size(a) for a in ("sx", "sy", "grp"))
    n_b = n_sx * n_grp
    seg = GROWS // n_sy
    gscale = 1.0 / math.sqrt(S * n_sx * n_sy * n_grp * CX * CY)
    vmem = pl.BlockSpec(memory_space=pltpu.VMEM)
    smem = pl.BlockSpec(memory_space=pltpu.SMEM)
    hbm = pl.BlockSpec(memory_space=pltpu.HBM)

    def buf(*shape, dtype=f32):
        return pltpu.VMEM(shape, dtype)

    def sems(count):
        return pltpu.SemaphoreType.DMA((count,))

    outs = pl.pallas_call(
        functools.partial(kernel, n_sx, n_sy, n_grp, gscale),
        out_shape=[
            jax.ShapeDtypeStruct((3 * PZ * CX, CY), f32),
            jax.ShapeDtypeStruct((27, 128), f32),
            jax.ShapeDtypeStruct((1, 128), f32),
            jax.ShapeDtypeStruct((128, 128), f32),
            jax.ShapeDtypeStruct((1, 128), f32),
            jax.ShapeDtypeStruct((6, 128), f32),
        ],
        in_specs=[hbm] * 2 + [vmem] * 5 + [smem, vmem],
        out_specs=[vmem] * 6,
        scratch_shapes=[
            buf(3 * PZ * CX, CY), buf(6 * PZ * CX, CY),
            buf(PZ * PLANE, CY), buf(PZ * PLANE, CY, dtype=bf16),
            buf(S * PLANE, CY), buf(S * PLANE, CY, dtype=bf16),
            buf(S * CX * TROW, CY),
            buf(PZ * TPLANE, CY),
            buf(128, 128, dtype=bf16), buf(144, 256, dtype=bf16), buf(16, 128, dtype=bf16),
            buf(128, 256, dtype=bf16),
            buf(128, 128, dtype=bf16), buf(128, 16, dtype=bf16),
            buf(128, 128), buf(256, 128),
            buf(2, 128, NC, dtype=bf16), buf(2, 128, NC, dtype=bf16), buf(2, 8, NC),
            buf(GROWS, 128),
            *[buf(S * PER, 128, NC, dtype=bf16) for _ in range(5)],
            buf(2, 24, CY), buf(CX, CY), buf(208, CY),
            buf(6 * CX, CY), buf(6 * CX, CY),
            buf(24, CY), buf(CX, CY),
            buf(2, 2, 24, CY), buf(2, CX, CY), buf(2, 112, CY), buf(CX, CY),
            buf(6 * CX, CY), buf(6 * CX, CY),
            buf(n_sy, seg, 128), buf(n_sy, seg, 128), buf(seg, 128),
            buf(n_b, seg, 128), buf(seg, 128), buf(n_sy, seg, 128),
            sems(2), sems(2), sems(2), sems(3), sems(3), sems(3), sems(3),
        ],
        compiler_params=pltpu.CompilerParams(
            collective_id=0, has_side_effects=True, vmem_limit_bytes=62 * 2**20
        ),
    )(
        velocity.reshape(3 * PZ * CX, CY),
        target_stress.reshape(6 * PZ * CX, CY),
        w_conv,
        b_conv.reshape(1, 128),
        w_mix,
        b_mix.reshape(1, 128),
        w_out.T,
        plane_offsets.reshape(S),
        trainer_map.reshape(1, n_sy * S),
    )
    outs = pl.pallas_call(
        write_out,
        out_shape=[jax.ShapeDtypeStruct(o.shape, o.dtype) for o in outs],
        in_specs=[vmem] * 6,
        out_specs=[vmem] * 6,
    )(*outs)
    return (
        outs[0].reshape(3, PZ, CX, CY),
        outs[1],
        outs[2].reshape(128),
        outs[3],
        outs[4].reshape(128),
        outs[5].T,
    )


def solution(mesh):
    in_specs = (
        P(None, "grp", "sx", "sy"),
        P(None, "grp", "sx", "sy"),
        P(),
        P(),
        P(),
        P(),
        P(),
        P("grp", "sx", "sy", None),
        P("grp", "sx", None, None),
    )
    out_specs = (P(None, "grp", "sx", "sy"), P(), P(), P(), P(), P())
    return jax.shard_map(shards, mesh=mesh, in_specs=in_specs, out_specs=out_specs, check_vma=False)
```

```python
import functools
import math

import jax
import jax.numpy as jnp
from jax import lax
from jax.experimental import pallas as pl
from jax.experimental.pallas import tpu as pltpu
from jax.sharding import PartitionSpec as P

f32 = jnp.float32
bf16 = jnp.bfloat16
MESH = pl.DeviceIdType.MESH
HIGH = lax.Precision.HIGHEST

S = 2
gelu_c = 0.7978845608
gelu_k = 0.044715
visc = 0.1
lam = (gelu_c * gelu_k) ** (1.0 / 3.0)
shift_c = gelu_c / lam

PZ = 8
CX = 32
CY = 128
BLK = 16
PLANE = (CX + 2) * BLK
TROW = 8
TPLANE = (CX + 2) * TROW
XC = 16
NC = XC * CY
PER = CX // XC
ORDER = (0, 7, 1, 2, 3, 4, 5, 6)
EARLY = 6
GROWS = 192

DX = (0, 3, 4)
DY = (3, 1, 5)
DZ = (4, 5, 2)


def dot(a, b, precision=None):
    return jnp.dot(a, b, preferred_element_type=f32, precision=precision)


def dot_nt(a, b, precision=None):
    return lax.dot_general(
        a, b, (((1,), (1,)), ((), ())), preferred_element_type=f32, precision=precision
    )


def split(value):
    high = value.astype(bf16).astype(f32)
    return high, value - high


def gate(m):
    return (m * jnp.tanh(m * (m * m + shift_c))).astype(bf16)


def gate_16(m):
    m = m.astype(bf16)
    return m * jnp.tanh(m * (m * m + bf16(shift_c)))


def gate_and_slope(m):
    m = m.astype(bf16)
    z = m * (m * m + bf16(shift_c))
    t = jnp.tanh(z)
    up = bf16(1.0) + t
    down = bf16(1.0) - t
    return m * up, up * (bf16(1.0) + down * (bf16(3.0) * z - bf16(2.0 * shift_c) * m))


def lanes(shape):
    return lax.broadcasted_iota(jnp.int32, shape, 1)


def rows(shape):
    return lax.broadcasted_iota(jnp.int32, shape, 0)


def load_patches(buffer, base, count):
    return jnp.concatenate(
        [
            buffer[pl.ds(pl.multiple_of(base + x * BLK, BLK), 3 * BLK), :]
            for x in range(count)
        ],
        axis=1,
    )


def kernel(
    n_sx, n_sy, n_grp, gscale,
    vel_in, tgt_in, wc, bc, wm, bm, wo, offs, tmap,
    tend, gconv, gbconv, gmix, gbmix, gout,
    vel, tgt,
    qf, qb, sf, sb, tg, stress, cw, mw, ow, tw2, wb2, wbo, prep, prep2,
    q1, q2, lin, grad, h1, d1, h2, d2, g2,
    rowsrc, colsrc, hdst, zsrc, zdst, hr, cc,
    srowsrc, scolsrc, edst, scc, szsrc, szdst,
    gseg, ra, part_a, rb, part_b, rc,
    ins, hs, hrv, ss, srv, rs, rr,
):
    isx, isy, igr = lax.axis_index("sx"), lax.axis_index("sy"), lax.axis_index("grp")
    up_x, down_x = lax.rem(isx + 1, n_sx), lax.rem(isx + n_sx - 1, n_sx)
    ys = (lax.rem(isy + n_sy - 1, n_sy), isy, lax.rem(isy + 1, n_sy))
    other = 1 - igr
    n_b = n_sx * n_grp
    ib = isx * n_grp + igr

    def in_sy(k):
        return lax.rem(isy + k, n_sy)

    def in_b(k):
        return lax.rem(ib + k, n_b)

    def at_sy(i):
        return (isx, i, igr)

    def at_b(i):
        return (i // n_grp, isy, lax.rem(i, n_grp))

    loads = [
        pltpu.make_async_copy(vel_in, vel, ins.at[0]),
        pltpu.make_async_copy(tgt_in, tgt, ins.at[1]),
    ]
    for copy in loads:
        copy.start()

    barrier = pltpu.get_barrier_semaphore()

    def greet(device):
        pl.semaphore_signal(barrier, inc=1, device_id=device, device_id_type=MESH)

    friends = [at_sy(in_sy(k)) for k in range(1, n_sy)]
    friends += [at_b(in_b(k)) for k in range(1, n_b)]
    friends += [(to_x, to_y, igr) for to_x in (up_x, down_x) for to_y in (ys[0], ys[2])]
    for device in friends:
        greet(device)

    def remote(src, dst, send, recv, device):
        return pltpu.make_async_remote_copy(
            src_ref=src, dst_ref=dst, send_sem=send, recv_sem=recv,
            device_id=device, device_id_type=MESH,
        )

    def all_of(buffer, send, recv):
        return remote(buffer, buffer, send, recv, at_sy(in_sy(1)))

    prep[...] = jnp.zeros(prep.shape, f32)
    for c in range(3):
        for a in range(3):
            prep[a * BLK + c * 3 : a * BLK + c * 3 + 3, :] = wc[
                c * 9 + 3 * a : c * 9 + 3 * a + 3, :
            ].astype(f32)
    prep[9:10, :] = bc[...]
    w1 = prep[...][0:48, :]
    w2h = wm[...].astype(f32) * 0.5
    row48 = rows((48, 128))
    conv_high, conv_low = split(w1 * lam)
    pad = jnp.zeros((32, 128), f32)
    cw[...] = jnp.concatenate([conv_high, conv_low, pad], axis=0).T.astype(bf16)
    comp = dot(w1 * lam, w2h, HIGH)
    comp = comp + jnp.where(row48 == 9, lam * bm[...], 0.0)
    comp_high, comp_low = split(comp)
    pick = (lanes((16, 6)) == rows((16, 6))) | (lanes((16, 6)) + 8 == rows((16, 6)))
    wo_rows = dot(pick.astype(bf16), wo[...])
    ow[...] = jnp.where(rows((16, 128)) < 8, wo_rows, 0.0).astype(bf16)
    prep[...] = jnp.zeros(prep.shape, f32)
    prep[0:16, :] = wo_rows
    wo16 = prep[...].T[:, 0:16]
    outl = dot(jnp.concatenate([w2h, comp], axis=0), wo16, HIGH)
    out_high, out_low = split(outl)
    outl = jnp.where(lanes((176, 16)) < 8, out_high, out_low)
    mw[0:128, 0:128] = w2h.T.astype(bf16)
    tail = jnp.concatenate([comp_high, comp_low, pad], axis=0)
    mw[0:128, 128:256] = tail.T.astype(bf16)
    prep2[...] = jnp.zeros(prep2.shape, f32)
    prep2[0:176, 0:16] = outl
    mw[128:144, 0:128] = prep2[0:128, :].T[0:16, :].astype(bf16)
    mw[128:144, 128:256] = prep2[128:256, :].T[0:16, :].astype(bf16)
    bh, rest = split(lam * bm[...])
    bmid, rest = split(rest)
    row128 = rows((128, 128))
    t2 = jnp.where(row128 == 9, bh, jnp.where(row128 == 10, bmid, jnp.where(row128 == 11, rest, 0.0)))
    tw2[:, 0:128] = w2h.T.astype(bf16)
    tw2[:, 128:256] = t2.T.astype(bf16)
    wb2[...] = w2h.astype(bf16)
    wbo[...] = (0.5 * jnp.where(lanes((128, 16)) < 8, wo16, 0.0)).astype(bf16)


    qf[...] = jnp.ones(qf.shape, f32)
    sf[...] = jnp.ones(sf.shape, f32)
    tg[...] = jnp.zeros(tg.shape, f32)
    grad[...] = jnp.zeros(grad.shape, f32)
    scolsrc[...] = jnp.zeros(scolsrc.shape, f32)
    srowsrc[...] = jnp.zeros(srowsrc.shape, f32)
    loads[0].wait()
    for c in range(3):
        for side, x in ((0, 0), (1, CX - 1)):
            rowsrc[side, 8 * c : 8 * c + 8, :] = vel[pl.ds(c * PZ * CX + x, PZ, stride=CX), :]
        for side, p in ((0, PZ - 1), (1, 0)):
            zsrc[(side * 3 + c) * CX : (side * 3 + c + 1) * CX, :] = vel[pl.ds((c * PZ + p) * CX, CX), :]
    lane = lanes((CX, CY))

    def pack_cols(p, acc):
        for c in range(3):
            j = c * PZ + p
            v = vel[pl.ds(pl.multiple_of(j * CX, CX), CX), :]
            acc = jnp.where(lane // 2 == j, pltpu.roll(v, 2 * j + 1, 1), acc)
        return acc

    colsrc[...] = lax.fori_loop(0, PZ, pack_cols, jnp.zeros((CX, CY), f32))

    halo = []
    for d in (-1, 0, 1):
        for side, to_x in ((0, up_x), (1, down_x)):
            slot = side * 3 + 1 - d
            halo.append(
                remote(
                    rowsrc.at[1 - side], hdst.at[pl.ds(slot * 24, 24)],
                    hs.at[0], hrv.at[0], (to_x, ys[1 + d], igr),
                )
            )
    for side, to_y in ((0, ys[2]), (1, ys[0])):
        halo.append(
            remote(
                colsrc, hdst.at[pl.ds(144 + side * CX, CX)],
                hs.at[0], hrv.at[0], (isx, to_y, igr),
            )
        )
    halo_all = all_of(hdst, hs.at[0], hrv.at[0])
    halo_z = remote(zsrc, zdst, hs.at[1], hrv.at[1], (isx, isy, other))

    def enter():
        pl.semaphore_wait(barrier, len(friends))
        for copy in halo:
            copy.start()
        halo_z.start()

    loads[1].wait()
    names = tmap[...]
    place = lanes(names.shape)

    def scale_of(s):
        dest = jnp.sum(jnp.where(place == isy * S + s, names, 0), axis=1, keepdims=True)
        count = jnp.sum((names == dest).astype(f32), axis=1, keepdims=True)
        return 2.0 * gscale / count

    scales = [scale_of(s) for s in range(S)]

    zero8 = jnp.zeros((8, 128), f32)
    for s in range(S):
        chosen = lax.broadcasted_iota(jnp.int32, (PZ, CX, CY), 0) == offs[s]

        def plane(ref, c, chosen=chosen):
            stack = ref[c * PZ * CX : (c + 1) * PZ * CX, :].reshape(PZ, CX, CY)
            return jnp.sum(jnp.where(chosen, stack, 0.0), axis=0)

        for side in (0, CX + 1):
            at = s * PLANE + side * BLK
            sf[at : at + 8, :] = zero8
            sf[at + 8 : at + 9, :] = zero8[0:1]
        for c in range(3):
            v = plane(vel, c)
            for b in range(3):
                if b == 0:
                    w = jnp.where(lane == 0, 0.0, pltpu.roll(v, 1, 1))
                elif b == 2:
                    w = jnp.where(lane == CY - 1, 0.0, pltpu.roll(v, CY - 1, 1))
                else:
                    w = v
                sf[pl.ds(s * PLANE + BLK + c * 3 + b, CX, stride=BLK), :] = w
        for c in range(6):
            tg[pl.ds(s * CX * TROW + c, CX, stride=TROW), :] = scales[s] * plane(tgt, c)
    sb[...] = sf[...].astype(bf16)

    def sample_patches(k):
        s, part = k // PER, k % PER
        return load_patches(sb, s * PLANE + part * (XC * BLK), XC)

    def train_conv(k):
        pats = sample_patches(k)
        m = dot(cw[:, 0:96], jnp.concatenate([pats, pats], axis=0))
        h1[k], d1[k] = gate_and_slope(m)

    def train_mix(k):
        pats = sample_patches(k)
        h2[k], d2[k] = gate_and_slope(
            dot(tw2[:, 0:144], jnp.concatenate([h1[k], pats[0:16]], axis=0))
        )

    def train_out(k):
        s, part = k // PER, k % PER
        tau = dot(ow[...], h2[k])[0:8] * (scales[s] * (0.5 / lam))
        at = s * (CX * TROW) + part * (XC * TROW)
        target = jnp.concatenate(
            [tg[at + x * TROW : at + (x + 1) * TROW, :] for x in range(XC)], axis=1
        )
        err = jnp.concatenate([tau - target, jnp.zeros((8, NC), f32)], axis=0).astype(bf16)
        g2[k] = dot(wbo[...], err).astype(bf16) * d2[k]
        grad[176:184, :] += dot_nt(err, h2[k])[0:8]

    def train_back(k):
        pats = sample_patches(k)
        g1 = dot(wb2[...], g2[k]).astype(bf16) * d1[k]
        mix = dot_nt(jnp.concatenate([h1[k], pats[0:16]], axis=0), g2[k])
        grad[0:128, :] += mix[0:128]
        grad[184:192, :] += mix[136:144]
        grad[128:176, :] += dot_nt(pats, g1)

    parts = S * PER
    for k in range(parts + 3):
        if 0 <= k - 3:
            train_back(k - 3)
        if 0 <= k - 2 < parts:
            train_out(k - 2)
        if 0 <= k - 1 < parts:
            train_mix(k - 1)
        if k < parts:
            train_conv(k)
        if k == 2:
            enter()
    grad[0:128, :] = grad[0:128, :] * (0.5 / lam)
    grad[176:184, :] = grad[176:184, :] * (0.5 / lam)

    seg = GROWS // n_sy
    for j in range(n_sy):
        gseg[j] = grad[j * seg : (j + 1) * seg, :]
    scatter = [
        remote(gseg.at[in_sy(k)], ra.at[isy], rs.at[0], rr.at[0], at_sy(in_sy(k)))
        for k in range(1, n_sy)
    ]
    scatter_all = all_of(ra.at[pl.ds(0, n_sy - 1)], rs.at[0], rr.at[0])
    wide = [
        remote(part_a, rb.at[ib], rs.at[1], rr.at[1], at_b(in_b(k))) for k in range(1, n_b)
    ]
    wide_all = all_of(rb.at[pl.ds(0, n_b - 1)], rs.at[1], rr.at[1])
    gather = [
        remote(part_b, rc.at[isy], rs.at[2], rr.at[2], at_sy(in_sy(k))) for k in range(1, n_sy)
    ]
    gather_all = all_of(rc.at[pl.ds(0, n_sy - 1)], rs.at[2], rr.at[2])

    def total_of(buffer, count):
        total = buffer[0]
        for j in range(1, count):
            total = total + buffer[j]
        return total

    ra[isy] = gseg[isy]
    for copy in scatter:
        copy.start()

    def second():
        scatter_all.wait_recv()
        total = total_of(ra, n_sy)
        part_a[...] = total
        rb[ib] = total
        for copy in wide:
            copy.start()

    def third():
        wide_all.wait_recv()
        total = total_of(rb, n_b)
        part_b[...] = total
        rc[isy] = total
        for copy in gather:
            copy.start()

    halo_all.wait_recv()
    lane24 = lanes((24, CY))
    for side in (0, 1):
        left, mid, right = (hdst[(side * 3 + i) * 24 : (side * 3 + i + 1) * 24, :] for i in range(3))
        shifted = (
            jnp.where(lane24 == 0, pltpu.roll(left, 1, 1), pltpu.roll(mid, 1, 1)),
            mid,
            jnp.where(
                lane24 == CY - 1, pltpu.roll(right, CY - 1, 1), pltpu.roll(mid, CY - 1, 1)
            ),
        )
        at = side * (CX + 1) * BLK
        for b in range(3):
            hr[...] = shifted[b]
            for c in range(3):
                qf[pl.ds(at + c * 3 + b, PZ, stride=PLANE), :] = hr[8 * c : 8 * c + 8, :]
    cc[...] = jnp.where(
        lax.rem(lane, 2) == 0, pltpu.roll(hdst[176:208, :], CY - 1, 1), pltpu.roll(hdst[144:176, :], 1, 1)
    )

    def build(p):
        for c in range(3):
            j = c * PZ + p
            v = vel[pl.ds(pl.multiple_of(j * CX, CX), CX), :]
            edge = pltpu.roll(cc[...], CY - 1 - 2 * j, 1)
            at = p * PLANE + BLK + c * 3
            qf[pl.ds(at, CX, stride=BLK), :] = jnp.where(lane == 0, edge, pltpu.roll(v, 1, 1))
            qf[pl.ds(at + 1, CX, stride=BLK), :] = v
            qf[pl.ds(at + 2, CX, stride=BLK), :] = jnp.where(
                lane == CY - 1, edge, pltpu.roll(v, CY - 1, 1)
            )
        base = pl.ds(pl.multiple_of(p * PLANE, BLK), PLANE)
        qb[base, :] = qf[base, :].astype(bf16)

    def patches_of(k):
        return load_patches(qb, ORDER[k // PER] * PLANE + (k % PER) * (XC * BLK), XC)

    def stage_conv(k):
        pats = patches_of(k)
        q1[k % 2] = gate_16(dot(cw[:, 0:96], jnp.concatenate([pats, pats], axis=0)))

    def stage_mix(k):
        pats = patches_of(k)
        m2 = dot(mw[:, 0:224], jnp.concatenate([q1[k % 2], pats, pats], axis=0))
        q2[k % 2] = gate(m2[0:128])
        lin[k % 2] = m2[128:136] + m2[136:144]

    def stage_out(k):
        tau = dot(ow[...], q2[k % 2])[0:8] + lin[k % 2]
        at = ORDER[k // PER] * TPLANE + (k % PER * XC + 1) * TROW
        for x in range(XC):
            stress[at + x * TROW : at + (x + 1) * TROW, :] = tau[:, x * CY : (x + 1) * CY]

    zs = remote(szsrc, szdst, ss.at[2], srv.at[2], (isx, isy, other))

    def send_z():
        for side, p in ((0, PZ - 1), (1, 0)):
            for c in range(3):
                at = (side * 3 + c) * CX
                szsrc[at : at + CX, :] = stress[
                    pl.ds(p * TPLANE + TROW + DZ[c], CX, stride=TROW), :
                ]
        zs.start()


    def edge_copies(group):
        out = [
            remote(
                srowsrc.at[group, 1 - side], edst.at[group, pl.ds(side * 24, 24)],
                ss.at[group], srv.at[group], (to_x, isy, igr),
            )
            for side, to_x in ((0, up_x), (1, down_x))
        ]
        return out + [
            remote(
                scolsrc.at[group], edst.at[group, pl.ds(48 + side * CX, CX)],
                ss.at[group], srv.at[group], (isx, to_y, igr),
            )
            for side, to_y in ((0, ys[2]), (1, ys[0]))
        ]

    edges = [edge_copies(0), edge_copies(1)]
    edges_all = [all_of(edst.at[g], ss.at[g], srv.at[g]) for g in (0, 1)]
    groups = (ORDER[:EARLY], ORDER[EARLY:])

    def send_edges(group):
        acc = jnp.zeros((CX, CY), f32)
        for p in groups[group]:
            for c in range(3):
                j = c * PZ + p
                at = p * TPLANE
                for side, x in ((0, 1), (1, CX)):
                    srowsrc[group, side, j : j + 1, :] = stress[
                        at + x * TROW + DX[c] : at + x * TROW + DX[c] + 1, :
                    ]
                v = stress[pl.ds(at + TROW + DY[c], CX, stride=TROW), :]
                acc = jnp.where(lane // 2 == j, pltpu.roll(v, 2 * j + 1, 1), acc)
        scolsrc[group] = acc
        for copy in edges[group]:
            copy.start()

    chunks = PZ * PER
    build(ORDER[0])
    for k in range(chunks + 2):
        if k % PER == 0 and k // PER + 1 < PZ:
            build(ORDER[k // PER + 1])
        if 0 <= k - 2:
            stage_out(k - 2)
        if 0 <= k - 1 < chunks:
            stage_mix(k - 1)
        if k < chunks:
            stage_conv(k)
        if k == 14:
            send_z()
        if k - 2 == EARLY * PER - 1:
            send_edges(0)
        if k == 6:
            second()
        if k == 13:
            third()
    send_edges(1)

    halo_z.wait_recv()

    def viscous(p, below, above):
        for c in range(3):
            at = p * PLANE + BLK + c * 3

            def pick_at(start):
                return qf[pl.ds(start, CX, stride=BLK), :]

            mid = pick_at(at + 1)
            total = pick_at(at) + pick_at(at + 2)
            total = total + pick_at(at + 1 - BLK) + pick_at(at + 1 + BLK)
            total = total + below(c) + above(c) - 6.0 * mid
            tend[pl.ds(pl.multiple_of((c * PZ + p) * CX, CX), CX), :] = visc * total

    def plane_of(p):
        return lambda c: vel[pl.ds(pl.multiple_of((c * PZ + p) * CX, CX), CX), :]

    def ghost(side):
        return lambda c: zdst[(side * 3 + c) * CX : (side * 3 + c + 1) * CX, :]

    viscous(0, ghost(0), plane_of(1))

    def inner(p, _):
        viscous(p, plane_of(p - 1), plane_of(p + 1))
        return 0

    lax.fori_loop(1, PZ - 1, inner, 0)
    viscous(PZ - 1, plane_of(PZ - 2), ghost(1))

    half = 0.25 / lam

    def diverge(p):
        for c in range(3):
            j = c * PZ + p

            def pick_at(plane, x, comp):
                if plane < 0 or plane == PZ:
                    side = 0 if plane < 0 else 1
                    return szdst[(side * 3 + c) * CX : (side * 3 + c + 1) * CX, :]
                return stress[pl.ds(plane * TPLANE + x * TROW + comp, CX, stride=TROW), :]

            along_x = pick_at(p, 2, DX[c]) - pick_at(p, 0, DX[c])
            v = pick_at(p, 1, DY[c])
            edge = pltpu.roll(scc[...], CY - 1 - 2 * j, 1)
            along_y = jnp.where(lane == CY - 1, edge, pltpu.roll(v, CY - 1, 1)) - jnp.where(
                lane == 0, edge, pltpu.roll(v, 1, 1)
            )
            along_z = pick_at(p + 1, 1, DZ[c]) - pick_at(p - 1, 1, DZ[c])
            at = pl.ds(j * CX, CX)
            tend[at, :] = tend[at, :] - half * (along_x + along_y + along_z)

    zs.wait_recv()
    for group in (0, 1):
        edges_all[group].wait_recv()
        for p in groups[group]:
            for side in (0, 1):
                for c in range(3):
                    at = p * TPLANE + side * (CX + 1) * TROW + DX[c]
                    stress[at : at + 1, :] = edst[
                        group, side * 24 + c * PZ + p : side * 24 + c * PZ + p + 1, :
                    ]
        scc[...] = jnp.where(
            lax.rem(lane, 2) == 0,
            pltpu.roll(edst[group, 80:112, :], CY - 1, 1),
            pltpu.roll(edst[group, 48:80, :], 1, 1),
        )
        for p in groups[group]:
            diverge(p)

    gather_all.wait_recv()
    for j in range(n_sy):
        grad[j * seg : (j + 1) * seg, :] = rc[j]
    gmix[...] = grad[0:128, :]
    for c in range(3):
        for a in range(3):
            at = 128 + a * BLK + c * 3
            gconv[c * 9 + 3 * a : c * 9 + 3 * a + 3, :] = grad[at : at + 3, :]
    gbconv[...] = grad[137:138, :]
    gbmix[...] = grad[185:186, :]
    gout[...] = grad[176:182, :]

    for group in (halo_all, halo_z, zs, *edges_all, scatter_all, wide_all, gather_all):
        group.wait_send()


def write_out(*refs):
    for source, result in zip(refs[:6], refs[6:]):
        result[...] = source[...]


def shards(velocity, target_stress, w_conv, b_conv, w_mix, b_mix, w_out, plane_offsets, trainer_map):
    n_sx, n_sy, n_grp = (lax.axis_size(a) for a in ("sx", "sy", "grp"))
    n_b = n_sx * n_grp
    seg = GROWS // n_sy
    gscale = 1.0 / math.sqrt(S * n_sx * n_sy * n_grp * CX * CY)
    vmem = pl.BlockSpec(memory_space=pltpu.VMEM)
    smem = pl.BlockSpec(memory_space=pltpu.SMEM)
    hbm = pl.BlockSpec(memory_space=pltpu.HBM)

    def buf(*shape, dtype=f32):
        return pltpu.VMEM(shape, dtype)

    def sems(count):
        return pltpu.SemaphoreType.DMA((count,))

    outs = pl.pallas_call(
        functools.partial(kernel, n_sx, n_sy, n_grp, gscale),
        out_shape=[
            jax.ShapeDtypeStruct((3 * PZ * CX, CY), f32),
            jax.ShapeDtypeStruct((27, 128), f32),
            jax.ShapeDtypeStruct((1, 128), f32),
            jax.ShapeDtypeStruct((128, 128), f32),
            jax.ShapeDtypeStruct((1, 128), f32),
            jax.ShapeDtypeStruct((6, 128), f32),
        ],
        in_specs=[hbm] * 2 + [vmem] * 5 + [smem, vmem],
        out_specs=[vmem] * 6,
        scratch_shapes=[
            buf(3 * PZ * CX, CY), buf(6 * PZ * CX, CY),
            buf(PZ * PLANE, CY), buf(PZ * PLANE, CY, dtype=bf16),
            buf(S * PLANE, CY), buf(S * PLANE, CY, dtype=bf16),
            buf(S * CX * TROW, CY),
            buf(PZ * TPLANE, CY),
            buf(128, 128, dtype=bf16), buf(144, 256, dtype=bf16), buf(16, 128, dtype=bf16),
            buf(128, 256, dtype=bf16),
            buf(128, 128, dtype=bf16), buf(128, 16, dtype=bf16),
            buf(128, 128), buf(256, 128),
            buf(2, 128, NC, dtype=bf16), buf(2, 128, NC, dtype=bf16), buf(2, 8, NC),
            buf(GROWS, 128),
            *[buf(S * PER, 128, NC, dtype=bf16) for _ in range(5)],
            buf(2, 24, CY), buf(CX, CY), buf(208, CY),
            buf(6 * CX, CY), buf(6 * CX, CY),
            buf(24, CY), buf(CX, CY),
            buf(2, 2, 24, CY), buf(2, CX, CY), buf(2, 112, CY), buf(CX, CY),
            buf(6 * CX, CY), buf(6 * CX, CY),
            buf(n_sy, seg, 128), buf(n_sy, seg, 128), buf(seg, 128),
            buf(n_b, seg, 128), buf(seg, 128), buf(n_sy, seg, 128),
            sems(2), sems(2), sems(2), sems(3), sems(3), sems(3), sems(3),
        ],
        compiler_params=pltpu.CompilerParams(
            collective_id=0, has_side_effects=True, vmem_limit_bytes=62 * 2**20
        ),
    )(
        velocity.reshape(3 * PZ * CX, CY),
        target_stress.reshape(6 * PZ * CX, CY),
        w_conv,
        b_conv.reshape(1, 128),
        w_mix,
        b_mix.reshape(1, 128),
        w_out.T,
        plane_offsets.reshape(S),
        trainer_map.reshape(1, n_sy * S),
    )
    outs = pl.pallas_call(
        write_out,
        out_shape=[jax.ShapeDtypeStruct(o.shape, o.dtype) for o in outs],
        in_specs=[vmem] * 6,
        out_specs=[vmem] * 6,
    )(*outs)
    return (
        outs[0].reshape(3, PZ, CX, CY),
        outs[1],
        outs[2].reshape(128),
        outs[3],
        outs[4].reshape(128),
        outs[5].T,
    )


def solution(mesh):
    in_specs = (
        P(None, "grp", "sx", "sy"),
        P(None, "grp", "sx", "sy"),
        P(),
        P(),
        P(),
        P(),
        P(),
        P("grp", "sx", "sy", None),
        P("grp", "sx", None, None),
    )
    out_specs = (P(None, "grp", "sx", "sy"), P(), P(), P(), P(), P())
    return jax.shard_map(shards, mesh=mesh, in_specs=in_specs, out_specs=out_specs, check_vma=False)
```

```python
import functools
import math

import jax
import jax.numpy as jnp
from jax import lax
from jax.experimental import pallas as pl
from jax.experimental.pallas import tpu as pltpu
from jax.sharding import PartitionSpec as P

f32 = jnp.float32
bf16 = jnp.bfloat16
MESH = pl.DeviceIdType.MESH
HIGH = lax.Precision.HIGHEST

S = 2
gelu_c = 0.7978845608
gelu_k = 0.044715
visc = 0.1
lam = (gelu_c * gelu_k) ** (1.0 / 3.0)
shift_c = gelu_c / lam

PZ = 8
CX = 32
CY = 128
BLK = 16
PLANE = (CX + 2) * BLK
TROW = 8
TPLANE = (CX + 2) * TROW
XC = 16
NC = XC * CY
PER = CX // XC
ORDER = (0, 7, 1, 2, 3, 4, 5, 6)
EARLY = 6
GROWS = 192

DX = (0, 3, 4)
DY = (3, 1, 5)
DZ = (4, 5, 2)


def dot(a, b, precision=None):
    return jnp.dot(a, b, preferred_element_type=f32, precision=precision)


def dot_nt(a, b, precision=None):
    return lax.dot_general(
        a, b, (((1,), (1,)), ((), ())), preferred_element_type=f32, precision=precision
    )


def split(value):
    high = value.astype(bf16).astype(f32)
    return high, value - high


def gate(m):
    return (m * jnp.tanh(m * (m * m + shift_c))).astype(bf16)


def gate_16(m):
    m = m.astype(bf16)
    return m * jnp.tanh(m * (m * m + bf16(shift_c)))


def gate_and_slope(m):
    m = m.astype(bf16)
    z = m * (m * m + bf16(shift_c))
    t = jnp.tanh(z)
    up = bf16(1.0) + t
    down = bf16(1.0) - t
    return m * up, up * (bf16(1.0) + down * (bf16(3.0) * z - bf16(2.0 * shift_c) * m))


def lanes(shape):
    return lax.broadcasted_iota(jnp.int32, shape, 1)


def rows(shape):
    return lax.broadcasted_iota(jnp.int32, shape, 0)


def load_patches(buffer, base, count):
    return jnp.concatenate(
        [
            buffer[pl.ds(pl.multiple_of(base + x * BLK, BLK), 3 * BLK), :]
            for x in range(count)
        ],
        axis=1,
    )


def kernel(
    n_sx, n_sy, n_grp, gscale,
    vel_in, tgt_in, wc, bc, wm, bm, wo, offs, tmap,
    tend, gconv, gbconv, gmix, gbmix, gout,
    vel, tgt,
    qf, qb, sf, sb, tg, stress, cw, mw, ow, tw2, wb2, wbo, prep, prep2,
    q1, q2, lin, grad, h1, d1, h2, d2, g2,
    rowsrc, colsrc, hdst, zsrc, zdst, hr, cc,
    srowsrc, scolsrc, edst, scc, szsrc, szdst,
    gseg, ra, part_a, rb, part_b, rc,
    ins, hs, hrv, ss, srv, rs, rr,
):
    isx, isy, igr = lax.axis_index("sx"), lax.axis_index("sy"), lax.axis_index("grp")
    up_x, down_x = lax.rem(isx + 1, n_sx), lax.rem(isx + n_sx - 1, n_sx)
    ys = (lax.rem(isy + n_sy - 1, n_sy), isy, lax.rem(isy + 1, n_sy))
    other = 1 - igr
    n_b = n_sx * n_grp
    ib = isx * n_grp + igr

    def in_sy(k):
        return lax.rem(isy + k, n_sy)

    def in_b(k):
        return lax.rem(ib + k, n_b)

    def at_sy(i):
        return (isx, i, igr)

    def at_b(i):
        return (i // n_grp, isy, lax.rem(i, n_grp))

    loads = [
        pltpu.make_async_copy(vel_in, vel, ins.at[0]),
        pltpu.make_async_copy(tgt_in, tgt, ins.at[1]),
    ]
    for copy in loads:
        copy.start()

    barrier = pltpu.get_barrier_semaphore()

    def greet(device):
        pl.semaphore_signal(barrier, inc=1, device_id=device, device_id_type=MESH)

    friends = [at_sy(in_sy(k)) for k in range(1, n_sy)]
    friends += [at_b(in_b(k)) for k in range(1, n_b)]
    friends += [(to_x, to_y, igr) for to_x in (up_x, down_x) for to_y in (ys[0], ys[2])]
    for device in friends:
        greet(device)

    def remote(src, dst, send, recv, device):
        return pltpu.make_async_remote_copy(
            src_ref=src, dst_ref=dst, send_sem=send, recv_sem=recv,
            device_id=device, device_id_type=MESH,
        )

    def all_of(buffer, send, recv):
        return remote(buffer, buffer, send, recv, at_sy(in_sy(1)))

    prep[...] = jnp.zeros(prep.shape, f32)
    for c in range(3):
        for a in range(3):
            prep[a * BLK + c * 3 : a * BLK + c * 3 + 3, :] = wc[
                c * 9 + 3 * a : c * 9 + 3 * a + 3, :
            ].astype(f32)
    prep[9:10, :] = bc[...]
    w1 = prep[...][0:48, :]
    w2h = wm[...].astype(f32) * 0.5
    row48 = rows((48, 128))
    conv_high, conv_low = split(w1 * lam)
    pad = jnp.zeros((32, 128), f32)
    cw[...] = jnp.concatenate([conv_high, conv_low, pad], axis=0).T.astype(bf16)
    comp = dot(w1 * lam, w2h, HIGH)
    comp = comp + jnp.where(row48 == 9, lam * bm[...], 0.0)
    comp_high, comp_low = split(comp)
    pick = (lanes((16, 6)) == rows((16, 6))) | (lanes((16, 6)) + 8 == rows((16, 6)))
    wo_rows = dot(pick.astype(bf16), wo[...])
    ow[...] = jnp.where(rows((16, 128)) < 8, wo_rows, 0.0).astype(bf16)
    prep[...] = jnp.zeros(prep.shape, f32)
    prep[0:16, :] = wo_rows
    wo16 = prep[...].T[:, 0:16]
    outl = dot(jnp.concatenate([w2h, comp], axis=0), wo16, HIGH)
    out_high, out_low = split(outl)
    outl = jnp.where(lanes((176, 16)) < 8, out_high, out_low)
    mw[0:128, 0:128] = w2h.T.astype(bf16)
    tail = jnp.concatenate([comp_high, comp_low, pad], axis=0)
    mw[0:128, 128:256] = tail.T.astype(bf16)
    prep2[...] = jnp.zeros(prep2.shape, f32)
    prep2[0:176, 0:16] = outl
    mw[128:144, 0:128] = prep2[0:128, :].T[0:16, :].astype(bf16)
    mw[128:144, 128:256] = prep2[128:256, :].T[0:16, :].astype(bf16)
    bh, rest = split(lam * bm[...])
    bmid, rest = split(rest)
    row128 = rows((128, 128))
    t2 = jnp.where(row128 == 9, bh, jnp.where(row128 == 10, bmid, jnp.where(row128 == 11, rest, 0.0)))
    tw2[:, 0:128] = w2h.T.astype(bf16)
    tw2[:, 128:256] = t2.T.astype(bf16)
    wb2[...] = w2h.astype(bf16)
    wbo[...] = (0.5 * jnp.where(lanes((128, 16)) < 8, wo16, 0.0)).astype(bf16)


    qf[...] = jnp.ones(qf.shape, f32)
    sf[...] = jnp.ones(sf.shape, f32)
    tg[...] = jnp.zeros(tg.shape, f32)
    grad[...] = jnp.zeros(grad.shape, f32)
    scolsrc[...] = jnp.zeros(scolsrc.shape, f32)
    srowsrc[...] = jnp.zeros(srowsrc.shape, f32)
    loads[0].wait()
    for c in range(3):
        for side, x in ((0, 0), (1, CX - 1)):
            rowsrc[side, 8 * c : 8 * c + 8, :] = vel[pl.ds(c * PZ * CX + x, PZ, stride=CX), :]
        for side, p in ((0, PZ - 1), (1, 0)):
            zsrc[(side * 3 + c) * CX : (side * 3 + c + 1) * CX, :] = vel[pl.ds((c * PZ + p) * CX, CX), :]
    lane = lanes((CX, CY))

    def pack_cols(p, acc):
        for c in range(3):
            j = c * PZ + p
            v = vel[pl.ds(pl.multiple_of(j * CX, CX), CX), :]
            acc = jnp.where(lane // 2 == j, pltpu.roll(v, 2 * j + 1, 1), acc)
        return acc

    colsrc[...] = lax.fori_loop(0, PZ, pack_cols, jnp.zeros((CX, CY), f32))

    halo = []
    for d in (-1, 0, 1):
        for side, to_x in ((0, up_x), (1, down_x)):
            slot = side * 3 + 1 - d
            halo.append(
                remote(
                    rowsrc.at[1 - side], hdst.at[pl.ds(slot * 24, 24)],
                    hs.at[0], hrv.at[0], (to_x, ys[1 + d], igr),
                )
            )
    for side, to_y in ((0, ys[2]), (1, ys[0])):
        halo.append(
            remote(
                colsrc, hdst.at[pl.ds(144 + side * CX, CX)],
                hs.at[0], hrv.at[0], (isx, to_y, igr),
            )
        )
    halo_all = all_of(hdst, hs.at[0], hrv.at[0])
    halo_z = remote(zsrc, zdst, hs.at[1], hrv.at[1], (isx, isy, other))

    def enter():
        pl.semaphore_wait(barrier, len(friends))
        for copy in halo:
            copy.start()
        halo_z.start()

    loads[1].wait()
    names = tmap[...]
    place = lanes(names.shape)

    def scale_of(s):
        dest = jnp.sum(jnp.where(place == isy * S + s, names, 0), axis=1, keepdims=True)
        count = jnp.sum((names == dest).astype(f32), axis=1, keepdims=True)
        return 2.0 * gscale / count

    scales = [scale_of(s) for s in range(S)]

    zero8 = jnp.zeros((8, 128), f32)
    for s in range(S):
        chosen = lax.broadcasted_iota(jnp.int32, (PZ, CX, CY), 0) == offs[s]

        def plane(ref, c, chosen=chosen):
            stack = ref[c * PZ * CX : (c + 1) * PZ * CX, :].reshape(PZ, CX, CY)
            return jnp.sum(jnp.where(chosen, stack, 0.0), axis=0)

        for side in (0, CX + 1):
            at = s * PLANE + side * BLK
            sf[at : at + 8, :] = zero8
            sf[at + 8 : at + 9, :] = zero8[0:1]
        for c in range(3):
            v = plane(vel, c)
            for b in range(3):
                if b == 0:
                    w = jnp.where(lane == 0, 0.0, pltpu.roll(v, 1, 1))
                elif b == 2:
                    w = jnp.where(lane == CY - 1, 0.0, pltpu.roll(v, CY - 1, 1))
                else:
                    w = v
                sf[pl.ds(s * PLANE + BLK + c * 3 + b, CX, stride=BLK), :] = w
        for c in range(6):
            tg[pl.ds(s * CX * TROW + c, CX, stride=TROW), :] = scales[s] * plane(tgt, c)
    sb[...] = sf[...].astype(bf16)

    def sample_patches(k):
        s, part = k // PER, k % PER
        return load_patches(sb, s * PLANE + part * (XC * BLK), XC)

    def train_conv(k):
        pats = sample_patches(k)
        m = dot(cw[:, 0:96], jnp.concatenate([pats, pats], axis=0))
        h1[k], d1[k] = gate_and_slope(m)

    def train_mix(k):
        pats = sample_patches(k)
        h2[k], d2[k] = gate_and_slope(
            dot(tw2[:, 0:144], jnp.concatenate([h1[k], pats[0:16]], axis=0))
        )

    def train_out(k):
        s, part = k // PER, k % PER
        tau = dot(ow[...], h2[k])[0:8] * (scales[s] * (0.5 / lam))
        at = s * (CX * TROW) + part * (XC * TROW)
        target = jnp.concatenate(
            [tg[at + x * TROW : at + (x + 1) * TROW, :] for x in range(XC)], axis=1
        )
        err = jnp.concatenate([tau - target, jnp.zeros((8, NC), f32)], axis=0).astype(bf16)
        g2[k] = dot(wbo[...], err).astype(bf16) * d2[k]
        grad[176:184, :] += dot_nt(err, h2[k])[0:8]

    def train_back(k):
        pats = sample_patches(k)
        g1 = dot(wb2[...], g2[k]).astype(bf16) * d1[k]
        mix = dot_nt(jnp.concatenate([h1[k], pats[0:16]], axis=0), g2[k])
        grad[0:128, :] += mix[0:128]
        grad[184:192, :] += mix[136:144]
        grad[128:176, :] += dot_nt(pats, g1)

    parts = S * PER
    for k in range(parts + 3):
        if 0 <= k - 3:
            train_back(k - 3)
        if 0 <= k - 2 < parts:
            train_out(k - 2)
        if 0 <= k - 1 < parts:
            train_mix(k - 1)
        if k < parts:
            train_conv(k)
        if k == 2:
            enter()
    grad[0:128, :] = grad[0:128, :] * (0.5 / lam)
    grad[176:184, :] = grad[176:184, :] * (0.5 / lam)

    seg = GROWS // n_sy
    for j in range(n_sy):
        gseg[j] = grad[j * seg : (j + 1) * seg, :]
    scatter = [
        remote(gseg.at[in_sy(k)], ra.at[isy], rs.at[0], rr.at[0], at_sy(in_sy(k)))
        for k in range(1, n_sy)
    ]
    scatter_all = all_of(ra.at[pl.ds(0, n_sy - 1)], rs.at[0], rr.at[0])
    wide = [
        remote(part_a, rb.at[ib], rs.at[1], rr.at[1], at_b(in_b(k))) for k in range(1, n_b)
    ]
    wide_all = all_of(rb.at[pl.ds(0, n_b - 1)], rs.at[1], rr.at[1])
    gather = [
        remote(part_b, rc.at[isy], rs.at[2], rr.at[2], at_sy(in_sy(k))) for k in range(1, n_sy)
    ]
    gather_all = all_of(rc.at[pl.ds(0, n_sy - 1)], rs.at[2], rr.at[2])

    def total_of(buffer, count):
        total = buffer[0]
        for j in range(1, count):
            total = total + buffer[j]
        return total

    ra[isy] = gseg[isy]
    for copy in scatter:
        copy.start()

    def second():
        scatter_all.wait_recv()
        total = total_of(ra, n_sy)
        part_a[...] = total
        rb[ib] = total
        for copy in wide:
            copy.start()

    def third():
        wide_all.wait_recv()
        total = total_of(rb, n_b)
        part_b[...] = total
        rc[isy] = total
        for copy in gather:
            copy.start()

    halo_all.wait_recv()
    lane24 = lanes((24, CY))
    for side in (0, 1):
        left, mid, right = (hdst[(side * 3 + i) * 24 : (side * 3 + i + 1) * 24, :] for i in range(3))
        shifted = (
            jnp.where(lane24 == 0, pltpu.roll(left, 1, 1), pltpu.roll(mid, 1, 1)),
            mid,
            jnp.where(
                lane24 == CY - 1, pltpu.roll(right, CY - 1, 1), pltpu.roll(mid, CY - 1, 1)
            ),
        )
        at = side * (CX + 1) * BLK
        for b in range(3):
            hr[...] = shifted[b]
            for c in range(3):
                qf[pl.ds(at + c * 3 + b, PZ, stride=PLANE), :] = hr[8 * c : 8 * c + 8, :]
    cc[...] = jnp.where(
        lax.rem(lane, 2) == 0, pltpu.roll(hdst[176:208, :], CY - 1, 1), pltpu.roll(hdst[144:176, :], 1, 1)
    )

    def build(p):
        for c in range(3):
            j = c * PZ + p
            v = vel[pl.ds(pl.multiple_of(j * CX, CX), CX), :]
            edge = pltpu.roll(cc[...], CY - 1 - 2 * j, 1)
            at = p * PLANE + BLK + c * 3
            qf[pl.ds(at, CX, stride=BLK), :] = jnp.where(lane == 0, edge, pltpu.roll(v, 1, 1))
            qf[pl.ds(at + 1, CX, stride=BLK), :] = v
            qf[pl.ds(at + 2, CX, stride=BLK), :] = jnp.where(
                lane == CY - 1, edge, pltpu.roll(v, CY - 1, 1)
            )
        base = pl.ds(pl.multiple_of(p * PLANE, BLK), PLANE)
        qb[base, :] = qf[base, :].astype(bf16)

    def patches_of(k):
        return load_patches(qb, ORDER[k // PER] * PLANE + (k % PER) * (XC * BLK), XC)

    def stage_conv(k):
        pats = patches_of(k)
        q1[k % 2] = gate_16(dot(cw[:, 0:96], jnp.concatenate([pats, pats], axis=0)))

    def stage_mix(k):
        pats = patches_of(k)
        m2 = dot(mw[:, 0:224], jnp.concatenate([q1[k % 2], pats, pats], axis=0))
        q2[k % 2] = gate(m2[0:128])
        lin[k % 2] = m2[128:136] + m2[136:144]

    def stage_out(k):
        tau = dot(ow[...], q2[k % 2])[0:8] + lin[k % 2]
        at = ORDER[k // PER] * TPLANE + (k % PER * XC + 1) * TROW
        for x in range(XC):
            stress[at + x * TROW : at + (x + 1) * TROW, :] = tau[:, x * CY : (x + 1) * CY]

    zs = remote(szsrc, szdst, ss.at[2], srv.at[2], (isx, isy, other))

    def send_z():
        for side, p in ((0, PZ - 1), (1, 0)):
            for c in range(3):
                at = (side * 3 + c) * CX
                szsrc[at : at + CX, :] = stress[
                    pl.ds(p * TPLANE + TROW + DZ[c], CX, stride=TROW), :
                ]
        zs.start()


    def edge_copies(group):
        out = [
            remote(
                srowsrc.at[group, 1 - side], edst.at[group, pl.ds(side * 24, 24)],
                ss.at[group], srv.at[group], (to_x, isy, igr),
            )
            for side, to_x in ((0, up_x), (1, down_x))
        ]
        return out + [
            remote(
                scolsrc.at[group], edst.at[group, pl.ds(48 + side * CX, CX)],
                ss.at[group], srv.at[group], (isx, to_y, igr),
            )
            for side, to_y in ((0, ys[2]), (1, ys[0]))
        ]

    edges = [edge_copies(0), edge_copies(1)]
    edges_all = [all_of(edst.at[g], ss.at[g], srv.at[g]) for g in (0, 1)]
    groups = (ORDER[:EARLY], ORDER[EARLY:])

    def send_edges(group):
        acc = jnp.zeros((CX, CY), f32)
        for p in groups[group]:
            for c in range(3):
                j = c * PZ + p
                at = p * TPLANE
                for side, x in ((0, 1), (1, CX)):
                    srowsrc[group, side, j : j + 1, :] = stress[
                        at + x * TROW + DX[c] : at + x * TROW + DX[c] + 1, :
                    ]
                v = stress[pl.ds(at + TROW + DY[c], CX, stride=TROW), :]
                acc = jnp.where(lane // 2 == j, pltpu.roll(v, 2 * j + 1, 1), acc)
        scolsrc[group] = acc
        for copy in edges[group]:
            copy.start()

    chunks = PZ * PER
    build(ORDER[0])
    for k in range(chunks + 2):
        if k % PER == 0 and k // PER + 1 < PZ:
            build(ORDER[k // PER + 1])
        if 0 <= k - 2:
            stage_out(k - 2)
        if 0 <= k - 1 < chunks:
            stage_mix(k - 1)
        if k < chunks:
            stage_conv(k)
        if k == 7:
            send_z()
        if k - 2 == EARLY * PER - 1:
            send_edges(0)
        if k == 6:
            second()
        if k == 13:
            third()
    send_edges(1)

    halo_z.wait_recv()

    def viscous(p, below, above):
        for c in range(3):
            at = p * PLANE + BLK + c * 3

            def pick_at(start):
                return qf[pl.ds(start, CX, stride=BLK), :]

            mid = pick_at(at + 1)
            total = pick_at(at) + pick_at(at + 2)
            total = total + pick_at(at + 1 - BLK) + pick_at(at + 1 + BLK)
            total = total + below(c) + above(c) - 6.0 * mid
            tend[pl.ds(pl.multiple_of((c * PZ + p) * CX, CX), CX), :] = visc * total

    def plane_of(p):
        return lambda c: vel[pl.ds(pl.multiple_of((c * PZ + p) * CX, CX), CX), :]

    def ghost(side):
        return lambda c: zdst[(side * 3 + c) * CX : (side * 3 + c + 1) * CX, :]

    viscous(0, ghost(0), plane_of(1))

    def inner(p, _):
        viscous(p, plane_of(p - 1), plane_of(p + 1))
        return 0

    lax.fori_loop(1, PZ - 1, inner, 0)
    viscous(PZ - 1, plane_of(PZ - 2), ghost(1))

    half = 0.25 / lam

    def diverge(p):
        for c in range(3):
            j = c * PZ + p

            def pick_at(plane, x, comp):
                if plane < 0 or plane == PZ:
                    side = 0 if plane < 0 else 1
                    return szdst[(side * 3 + c) * CX : (side * 3 + c + 1) * CX, :]
                return stress[pl.ds(plane * TPLANE + x * TROW + comp, CX, stride=TROW), :]

            along_x = pick_at(p, 2, DX[c]) - pick_at(p, 0, DX[c])
            v = pick_at(p, 1, DY[c])
            edge = pltpu.roll(scc[...], CY - 1 - 2 * j, 1)
            along_y = jnp.where(lane == CY - 1, edge, pltpu.roll(v, CY - 1, 1)) - jnp.where(
                lane == 0, edge, pltpu.roll(v, 1, 1)
            )
            along_z = pick_at(p + 1, 1, DZ[c]) - pick_at(p - 1, 1, DZ[c])
            at = pl.ds(j * CX, CX)
            tend[at, :] = tend[at, :] - half * (along_x + along_y + along_z)

    for group in (0, 1):
        edges_all[group].wait_recv()
        for p in groups[group]:
            for side in (0, 1):
                for c in range(3):
                    at = p * TPLANE + side * (CX + 1) * TROW + DX[c]
                    stress[at : at + 1, :] = edst[
                        group, side * 24 + c * PZ + p : side * 24 + c * PZ + p + 1, :
                    ]
        scc[...] = jnp.where(
            lax.rem(lane, 2) == 0,
            pltpu.roll(edst[group, 80:112, :], CY - 1, 1),
            pltpu.roll(edst[group, 48:80, :], 1, 1),
        )
        for p in groups[group]:
            if p not in (0, PZ - 1):
                diverge(p)
        if group == 0:
            zs.wait_recv()
            diverge(0)
            diverge(PZ - 1)

    gather_all.wait_recv()
    for j in range(n_sy):
        grad[j * seg : (j + 1) * seg, :] = rc[j]
    gmix[...] = grad[0:128, :]
    for c in range(3):
        for a in range(3):
            at = 128 + a * BLK + c * 3
            gconv[c * 9 + 3 * a : c * 9 + 3 * a + 3, :] = grad[at : at + 3, :]
    gbconv[...] = grad[137:138, :]
    gbmix[...] = grad[185:186, :]
    gout[...] = grad[176:182, :]

    for group in (halo_all, halo_z, zs, *edges_all, scatter_all, wide_all, gather_all):
        group.wait_send()


def write_out(*refs):
    for source, result in zip(refs[:6], refs[6:]):
        result[...] = source[...]


def shards(velocity, target_stress, w_conv, b_conv, w_mix, b_mix, w_out, plane_offsets, trainer_map):
    n_sx, n_sy, n_grp = (lax.axis_size(a) for a in ("sx", "sy", "grp"))
    n_b = n_sx * n_grp
    seg = GROWS // n_sy
    gscale = 1.0 / math.sqrt(S * n_sx * n_sy * n_grp * CX * CY)
    vmem = pl.BlockSpec(memory_space=pltpu.VMEM)
    smem = pl.BlockSpec(memory_space=pltpu.SMEM)
    hbm = pl.BlockSpec(memory_space=pltpu.HBM)

    def buf(*shape, dtype=f32):
        return pltpu.VMEM(shape, dtype)

    def sems(count):
        return pltpu.SemaphoreType.DMA((count,))

    outs = pl.pallas_call(
        functools.partial(kernel, n_sx, n_sy, n_grp, gscale),
        out_shape=[
            jax.ShapeDtypeStruct((3 * PZ * CX, CY), f32),
            jax.ShapeDtypeStruct((27, 128), f32),
            jax.ShapeDtypeStruct((1, 128), f32),
            jax.ShapeDtypeStruct((128, 128), f32),
            jax.ShapeDtypeStruct((1, 128), f32),
            jax.ShapeDtypeStruct((6, 128), f32),
        ],
        in_specs=[hbm] * 2 + [vmem] * 5 + [smem, vmem],
        out_specs=[vmem] * 6,
        scratch_shapes=[
            buf(3 * PZ * CX, CY), buf(6 * PZ * CX, CY),
            buf(PZ * PLANE, CY), buf(PZ * PLANE, CY, dtype=bf16),
            buf(S * PLANE, CY), buf(S * PLANE, CY, dtype=bf16),
            buf(S * CX * TROW, CY),
            buf(PZ * TPLANE, CY),
            buf(128, 128, dtype=bf16), buf(144, 256, dtype=bf16), buf(16, 128, dtype=bf16),
            buf(128, 256, dtype=bf16),
            buf(128, 128, dtype=bf16), buf(128, 16, dtype=bf16),
            buf(128, 128), buf(256, 128),
            buf(2, 128, NC, dtype=bf16), buf(2, 128, NC, dtype=bf16), buf(2, 8, NC),
            buf(GROWS, 128),
            *[buf(S * PER, 128, NC, dtype=bf16) for _ in range(5)],
            buf(2, 24, CY), buf(CX, CY), buf(208, CY),
            buf(6 * CX, CY), buf(6 * CX, CY),
            buf(24, CY), buf(CX, CY),
            buf(2, 2, 24, CY), buf(2, CX, CY), buf(2, 112, CY), buf(CX, CY),
            buf(6 * CX, CY), buf(6 * CX, CY),
            buf(n_sy, seg, 128), buf(n_sy, seg, 128), buf(seg, 128),
            buf(n_b, seg, 128), buf(seg, 128), buf(n_sy, seg, 128),
            sems(2), sems(2), sems(2), sems(3), sems(3), sems(3), sems(3),
        ],
        compiler_params=pltpu.CompilerParams(
            collective_id=0, has_side_effects=True, vmem_limit_bytes=62 * 2**20
        ),
    )(
        velocity.reshape(3 * PZ * CX, CY),
        target_stress.reshape(6 * PZ * CX, CY),
        w_conv,
        b_conv.reshape(1, 128),
        w_mix,
        b_mix.reshape(1, 128),
        w_out.T,
        plane_offsets.reshape(S),
        trainer_map.reshape(1, n_sy * S),
    )
    outs = pl.pallas_call(
        write_out,
        out_shape=[jax.ShapeDtypeStruct(o.shape, o.dtype) for o in outs],
        in_specs=[vmem] * 6,
        out_specs=[vmem] * 6,
    )(*outs)
    return (
        outs[0].reshape(3, PZ, CX, CY),
        outs[1],
        outs[2].reshape(128),
        outs[3],
        outs[4].reshape(128),
        outs[5].T,
    )


def solution(mesh):
    in_specs = (
        P(None, "grp", "sx", "sy"),
        P(None, "grp", "sx", "sy"),
        P(),
        P(),
        P(),
        P(),
        P(),
        P("grp", "sx", "sy", None),
        P("grp", "sx", None, None),
    )
    out_specs = (P(None, "grp", "sx", "sy"), P(), P(), P(), P(), P())
    return jax.shard_map(shards, mesh=mesh, in_specs=in_specs, out_specs=out_specs, check_vma=False)
```
